32 devices in a mesh: seq: 16 (over z, y, x), tp: 2 (over core).
Axes of the slice: x: 2, y: 2, z: 4, core: 2. Of those that a mesh axis runs over, the one named last changes fastest.
Arguments:
- queries: bfloat16 [2048, 3072], P('seq', 'tp'), may hold values from -6 to 6
- key_rows: bfloat16 [2048, 3072], P('seq', 'tp'), may hold values from -6 to 6
- value_rows: bfloat16 [2048, 3072], P('seq', 'tp'), may hold values from -6 to 6
- gate_input: bfloat16 [2048, 3072], P('seq', 'tp'), may hold values from -8 to 8
- norm_gain: float32 [3072], replicated, may hold values from 0.1 to 1.9
- doc_ids: int32 [2048], P('seq'), may hold values from 0 to 7, never falling along the last dimension, each value on 1 to 1024 neighbouring positions
- out_weight: bfloat16 [3072, 6144], P(None, 'tp'), may hold values from -0.109375 to 0.109375
Outputs:
- layer_out: bfloat16 [2048, 6144], P('seq', 'tp')
The draws below stay inside these ranges and needn't reach their ends.
Inputs may be any that keep to these rules, and one draw needn't show every extreme that they name: doc_ids never fall along the stream; every document id is used, each document has 1 to 1024 tokens and one has exactly 1024.
All inputs are finite; a program needn't handle non-finite values.
Results may differ from the reference program's by a relative error of at most 0.015.
Values may be sent and summed in bfloat16 or wider, within the bound.
No kernel may reach another device: no remote copies, remote signals or barrier semaphores. Data moves between devices by JAX's collectives and lax.ppermute only.
A program may use at most 64 MiB of HBM per device.

```python
import math
import jax
import jax.numpy as jnp
import numpy as np
from jax import lax

D = 6144
HEADS = 32
HD = 96
TOKENS = 2048
DOCS = 8
DOC_MOST = 1024


def levels(own_key, extent, split, smallest, top_value):
    def one(dim, blocks):
        steps = jax.random.uniform(jax.random.fold_in(jax.random.fold_in(own_key, 6), dim), (blocks,), jnp.float32, smallest / len(split), top_value / len(split))
        return jnp.repeat(jnp.exp(steps), extent[dim] // blocks).reshape((-1,) + (1,) * (len(extent) - dim - 1))

    factor_of = one(*split[0])
    for cut in split[1:]:
        factor_of = factor_of * one(*cut)
    return factor_of


def profile(number_of, total, bound, slope):
    loads = [(1 << 20) // math.isqrt(standing ** slope) + 1 for standing in range(2, number_of + 1)]
    spare, counts = total - bound - (number_of - 1), [1] * (number_of - 1)
    while spare > 0:
        free = [i for i in range(number_of - 1) if counts[i] < bound]
        whole, remaining = sum([loads[i] for i in free]), spare
        for i in free:
            addition = min(bound - counts[i], max(1, remaining * loads[i] // whole), spare)
            counts[i] = counts[i] + addition
            spare = spare - addition
    return np.array([bound] + counts)


def ragged_sizes(rng, number_of, total, most, slope):
    if number_of == 2:
        one = jax.random.randint(rng, (), max(1, total - most), min(most, total - 1) + 1)
        return jnp.stack([one, total - one])
    tallies = jnp.asarray(profile(number_of, total, most, slope), jnp.int32)
    pairs = (number_of - 1) // 2
    donor, sink = tallies[1:1 + 2 * pairs:2], tallies[2:2 + 2 * pairs:2]
    slack = jnp.minimum(donor - 1, most - sink)
    passed = jax.random.randint(jax.random.fold_in(rng, 1), (pairs,), 0, 1 << 20) % (slack + 1)
    tallies = tallies.at[1:1 + 2 * pairs:2].set(donor - passed).at[2:2 + 2 * pairs:2].set(sink + passed)
    return tallies[jax.random.permutation(jax.random.fold_in(rng, 2), number_of)]


def normal_values(own_key, extent, spread, bound, shards=(), kind=jnp.bfloat16):
    drawn = spread * jax.random.normal(own_key, extent, jnp.float32)
    if shards:
        drawn = drawn * levels(own_key, extent, shards, -0.22, 0.18)
    return jnp.clip(drawn, -bound, bound).astype(kind)


def setup_inputs(seed: int = 0) -> dict:
    key_list = jax.random.split(jax.random.key(seed), 8)
    return {
        "queries": normal_values(key_list[0], (TOKENS, HEADS * HD), 1.0, 6.0, ((0, 16), (1, 2))),
        "key_rows": normal_values(key_list[1], (TOKENS, HEADS * HD), 1.0, 6.0, ((0, 16), (1, 2))),
        "value_rows": normal_values(key_list[2], (TOKENS, HEADS * HD), 1.0, 6.0, ((0, 16), (1, 2))),
        "gate_input": normal_values(key_list[3], (TOKENS, HEADS * HD), 2.0, 8.0, ((0, 16), (1, 2))),
        "norm_gain": jnp.clip(1.0 + 0.18 * jax.random.normal(key_list[4], (HEADS * HD,), jnp.float32), 0.1, 1.9),
        "doc_ids": jnp.searchsorted(jnp.cumsum(ragged_sizes(key_list[5], DOCS, TOKENS, DOC_MOST, 0)), jnp.arange(TOKENS), side="right").astype(jnp.int32),
        "out_weight": normal_values(key_list[6], (HEADS * HD, D), (HEADS * HD) ** -0.5, 0.109375, ((1, 2),)),
    }


norm_eps = 1e-05

def reference(queries, key_rows, value_rows, gate_input, norm_gain, doc_ids, out_weight):
    width = HEADS * HD
    block = math.gcd(TOKENS, 512)
    count = TOKENS // block
    query_blocks = queries.reshape(count, block, HEADS, HD)
    key_blocks = key_rows.reshape(count, block, HEADS, HD)
    value_blocks = value_rows.reshape(count, block, HEADS, HD)
    doc_blocks = doc_ids.reshape(count, block)
    causal = jnp.arange(block)[:, None] >= jnp.arange(block)[None, :]
    highest = lax.Precision.HIGHEST

    def step(carry, item):
        state, carry_doc = carry
        query_b, key_b, value_b, doc_b = item
        query_f = query_b.astype(jnp.float32)
        key_f = key_b.astype(jnp.float32)
        value_f = value_b.astype(jnp.float32)
        scores = jnp.einsum('thd,shd->hts', query_f, key_f, precision=highest)
        keep = causal & (doc_b[:, None] == doc_b[None, :])
        scores = jnp.where(keep[None], scores, 0.0)
        intra = jnp.einsum('hts,shd->thd', scores, value_f, precision=highest)
        carried = jnp.einsum('thd,hde->the', query_f, state, precision=highest)
        attn = intra + jnp.where((doc_b == carry_doc)[:, None, None], carried, 0.0)
        last_doc = doc_b[-1]
        own_keys = jnp.where((doc_b == last_doc)[:, None, None], key_f, 0.0)
        own = jnp.einsum('thd,the->hde', own_keys, value_f, precision=highest)
        state = jnp.where(carry_doc == last_doc, state, 0.0) + own
        return ((state, last_doc), attn.reshape(block, width))
    init = (jnp.zeros((HEADS, HD, HD), jnp.float32), jnp.array(-1, jnp.int32))
    final, attn = lax.scan(step, init, (query_blocks, key_blocks, value_blocks, doc_blocks))
    attn = attn.reshape(TOKENS, width).astype(jnp.bfloat16)
    values = attn.astype(jnp.float32)
    scale = lax.rsqrt(lax.optimization_barrier(jnp.mean(values * values, axis=1)) + norm_eps)
    hidden = (values * scale[:, None] * norm_gain[None, :] * jax.nn.sigmoid(gate_input.astype(jnp.float32))).astype(jnp.bfloat16)
    return jnp.dot(hidden, out_weight, preferred_element_type=jnp.float32).astype(jnp.bfloat16)
```

```python
import functools

import jax
import jax.numpy as jnp
from jax import lax
from jax.experimental import pallas as pl
from jax.experimental.pallas import tpu as pltpu
from jax.sharding import PartitionSpec as P

HEADS = 32
HD = 96
WIDTH = HEADS * HD
DOC_MOST = 1024
UNIT = 4
UC = UNIT * HD
LANES = 128
SPLITS = 1
CUT = HD // SPLITS
BODY = CUT * (UC // LANES)
IDS = 16
PACKET = BODY + IDS
LOADS = 4
norm_eps = 1e-05

bf16 = jnp.bfloat16
f32 = jnp.float32
IN_VMEM = pl.BlockSpec(memory_space=pltpu.VMEM)
IN_HBM = pl.BlockSpec(memory_space=pltpu.HBM)


def call(kernel, outs, args, name, limit=16, scratch=(), far_in=(), far_out=(), flops=0, moved=0):
    args = [
        pltpu.with_memory_space_constraint(arg, pltpu.HBM) if i in far_in else arg
        for i, arg in enumerate(args)
    ]
    return pl.pallas_call(
        kernel,
        out_shape=outs,
        in_specs=[IN_HBM if i in far_in else IN_VMEM for i in range(len(args))],
        out_specs=[IN_HBM if i in far_out else IN_VMEM for i in range(len(outs))],
        scratch_shapes=list(scratch),
        compiler_params=pltpu.CompilerParams(vmem_limit_bytes=limit << 20),
        cost_estimate=pl.CostEstimate(flops=flops, bytes_accessed=moved, transcendentals=0),
        name=name,
    )(*args)


def fetch(pairs, sems):
    copies = [pltpu.make_async_copy(src, dst, sems.at[i]) for i, (src, dst) in enumerate(pairs)]
    for copy in copies:
        copy.start()
    return copies


def lane_head(shape):
    return lax.broadcasted_iota(jnp.int32, shape, 1) // HD


def diagonal(blocks, head):
    total = blocks[0]
    for a in range(1, UNIT):
        total = jnp.where(head == a, blocks[a], total)
    return total


def id_column(ids):
    rows = ids.shape[1]
    return jnp.broadcast_to(ids, (rows, rows)).T


def place_in(group):
    return lax.rem(lax.axis_index("seq"), group)


def rows_of(index, size):
    return pl.ds(pl.multiple_of(index * size, 16), size)


def own_kernel(group, key_hbm, value_hbm, doc_hbm, *refs):
    packets, (key_ref, value_ref, doc_ref, sems) = refs[:group], refs[group:]
    place = place_in(group)
    columns = []
    pairs = [(doc_hbm, doc_ref)]
    for i in range(group // SPLITS):
        unit = (place ^ (i * SPLITS)) // SPLITS
        cols = pl.ds(pl.multiple_of(unit * UC, LANES), UC)
        columns.append(cols)
        pairs += [(key_hbm.at[:, cols], key_ref.at[:, cols])]
        pairs += [(value_hbm.at[:, cols], value_ref.at[:, cols])]
    copies = fetch(pairs, sems)
    copies[0].wait()
    ids = doc_ref[...].astype(f32)
    first = jnp.min(ids, axis=1, keepdims=True)
    last = jnp.max(ids, axis=1, keepdims=True)
    keep = id_column(ids) == last
    keep = jnp.concatenate([keep] * (UC // keep.shape[1]), axis=1)
    head = lane_head((HD, UC))
    marks = jnp.where(
        lax.broadcasted_iota(jnp.int32, (IDS, LANES), 0) < IDS // 2,
        jnp.broadcast_to(last, (IDS, LANES)),
        jnp.broadcast_to(first, (IDS, LANES)),
    ).astype(bf16)
    for i, cols in enumerate(columns):
        copies[2 * i + 1].wait()
        copies[2 * i + 2].wait()
        keys = jnp.where(keep, key_ref[:, cols], jnp.zeros((), bf16))
        full = lax.dot_general(
            keys, value_ref[:, cols], (((0,), (0,)), ((), ())), preferred_element_type=f32
        )
        state = diagonal([full[a * HD : (a + 1) * HD] for a in range(UNIT)], head).astype(bf16)
        for s in range(SPLITS):
            out_ref = packets[i * SPLITS + s]
            part = state[:CUT]
            for r in range(1, SPLITS):
                mine = lax.rem(place ^ s, SPLITS) == r
                part = jnp.where(mine, state[r * CUT : (r + 1) * CUT], part)
            for c in range(UC // LANES):
                out_ref[c * CUT : (c + 1) * CUT] = part[:, c * LANES : (c + 1) * LANES]
            out_ref[BODY:] = marks


def read_packet(ref, base=0):
    marks = ref[base + BODY : base + PACKET].astype(f32)
    return ref[base : base + BODY].astype(f32), marks[0:1], marks[IDS // 2 : IDS // 2 + 1]


def group_kernel(group, beside_ref, *refs):
    packets, out_ref = [read_packet(ref) for ref in refs[:group]], refs[group]
    last = functools.reduce(jnp.maximum, [item[1] for item in packets])
    total = jnp.zeros((BODY, LANES), f32)
    for state, now, _ in packets:
        total = total + jnp.where(now == last, state, 0.0)
    out_ref[:BODY] = total.astype(bf16)
    out_ref[BODY:] = jnp.broadcast_to(last, (IDS, LANES)).astype(bf16)


def prefix_kernel(group, matchings, beside_ref, *refs):
    count = group + len(matchings)
    packets, earlier = refs[:group], refs[group:count]
    outs, (in_order, done) = refs[count:-2], refs[-2:]
    place = place_in(group)
    own_group = lax.axis_index("seq") // group
    for k in range(group):
        in_order[rows_of(place ^ k, PACKET)] = packets[k][...]
    own, last, first = read_packet(in_order)
    before = jnp.zeros((BODY, LANES), f32)
    for ref, (shift, odd) in zip(earlier, matchings):
        valid = jnp.where(lax.rem(own_group // shift, 2) == 1 - odd, 1.0, 0.0)
        state, now, _ = read_packet(ref)
        before = before + jnp.where(now == first, valid, 0.0) * state
    for j in range(group):
        if j:
            before_last = last
            through = own + jnp.where(last == first, before, 0.0)
            own, last, first = read_packet(in_order, j * PACKET)
            before = jnp.where(before_last == first, through, 0.0)
        done[j * BODY : (j + 1) * BODY] = before.astype(bf16)
    for k in range(group):
        outs[k][...] = done[rows_of(place ^ k, BODY)]


def start_load(weight_hbm, third, out_ref, sems):
    rows, columns = out_ref.shape
    step = rows // LOADS
    return fetch(
        [
            (
                weight_hbm.at[pl.ds(i * step, step), pl.ds(third * columns, columns)],
                out_ref.at[pl.ds(i * step, step)],
            )
            for i in range(LOADS)
        ],
        sems,
    )


def load_kernel(third, after_ref, weight_hbm, out_ref, sems):
    for copy in start_load(weight_hbm, third, out_ref, sems):
        copy.wait()


def intra_kernel(
    after_ref, query_hbm, key_hbm, value_hbm, gate_hbm, gain_hbm, doc_hbm, weight_hbm,
    intra_ref, scale_ref, open_ref, weight_ref,
    query_ref, key_ref, value_ref, gate_ref, gain_ref, doc_ref, sems, load_sems,
):
    rows, width = query_ref.shape
    copies = fetch(
        [
            (doc_hbm, doc_ref),
            (query_hbm, query_ref),
            (key_hbm, key_ref),
            (value_hbm, value_ref),
            (gain_hbm, gain_ref),
            (gate_hbm, gate_ref),
        ],
        sems,
    )
    loads = start_load(weight_hbm, 0, weight_ref, load_sems)
    copies[0].wait()
    ids = doc_ref[...].astype(f32)
    column = id_column(ids)
    causal = lax.broadcasted_iota(jnp.int32, (rows, rows), 0) >= lax.broadcasted_iota(
        jnp.int32, (rows, rows), 1
    )
    keep = jnp.concatenate([(column == ids) & causal] * UNIT, axis=0)
    opened = column == jnp.min(ids, axis=1, keepdims=True)
    opened = jnp.concatenate([opened] * (UC // rows), axis=1)
    head = lane_head((rows, UC))
    part = lax.axis_index("tp")
    for copy in copies[1:4]:
        copy.wait()
    for u in range(width // UC):
        cols = slice(u * UC, (u + 1) * UC)
        query = query_ref[:, cols]
        open_ref[:, cols] = jnp.where(opened, query, jnp.zeros((), bf16))
        stacked = jnp.concatenate(
            [jnp.where(head == a, query, jnp.zeros((), bf16)) for a in range(UNIT)], axis=0
        )
        scores = lax.dot_general(
            stacked, key_ref[:, cols], (((1,), (1,)), ((), ())), preferred_element_type=f32
        )
        scores = jnp.where(keep, scores, 0.0).astype(bf16)
        mixed = jnp.dot(scores, value_ref[:, cols], preferred_element_type=f32)
        intra_ref[:, cols] = diagonal(
            [mixed[a * rows : (a + 1) * rows] for a in range(UNIT)], head
        )
    copies[4].wait()
    copies[5].wait()
    for u in range(width // UC):
        cols = slice(u * UC, (u + 1) * UC)
        gain = gain_ref[:, pl.ds(pl.multiple_of(part * width + u * UC, LANES), UC)]
        scale_ref[:, cols] = gain * jax.nn.sigmoid(gate_ref[:, cols].astype(f32))
    for load in loads:
        load.wait()


def hidden_kernel(group, open_ref, intra_ref, scale_ref, beside_ref, *refs):
    states, (out_ref, in_order) = refs[:group], refs[group:]
    rows, width = open_ref.shape
    place = place_in(group)
    for k in range(group):
        in_order[rows_of(place ^ k, BODY)] = states[k][...]
    head = lane_head((HD, UC))
    squares = jnp.zeros((rows, LANES), f32)
    for u in range(width // UC):
        cols = slice(u * UC, (u + 1) * UC)
        pieces = []
        for s in range(SPLITS):
            base = (u * SPLITS + s) * BODY
            pieces.append(
                jnp.concatenate(
                    [
                        in_order[base + c * CUT : base + (c + 1) * CUT]
                        for c in range(UC // LANES)
                    ],
                    axis=1,
                )
            )
        state = jnp.concatenate(pieces, axis=0)
        spread = jnp.concatenate(
            [jnp.where(head == a, state, jnp.zeros((), bf16)) for a in range(UNIT)], axis=0
        )
        carried = jnp.dot(open_ref[:, cols], spread, preferred_element_type=f32)
        attn = (intra_ref[:, cols] + carried).astype(bf16).astype(f32)
        power = attn * attn
        for c in range(UC // LANES):
            squares = squares + power[:, c * LANES : (c + 1) * LANES]
        out_ref[:, cols] = (attn * scale_ref[:, cols]).astype(bf16)
    total = jnp.broadcast_to(jnp.sum(squares, axis=1, keepdims=True), (rows, LANES))
    high = total.astype(bf16)
    out_ref[:, width : width + LANES] = high
    out_ref[:, width + LANES :] = (total - high.astype(f32)).astype(bf16)


def near_kernel(hidden_ref, *refs):
    *weights, out_ref = refs
    depth = hidden_ref.shape[1] - 2 * LANES
    rows = pl.ds(pl.multiple_of(lax.axis_index("tp") * depth, LANES), depth)
    wide = weights[0].shape[1]
    for i, weight in enumerate(weights):
        out_ref[:, i * wide : (i + 1) * wide] = jnp.dot(
            hidden_ref[:, :depth], weight[rows], preferred_element_type=f32
        )


def far_kernel(parts, near_ref, *refs):
    weights, hidden, (out_hbm, out_ref, sems) = refs[:3], refs[3:-3], refs[-3:]
    depth = hidden[0].shape[1] - 2 * LANES
    wide = weights[0].shape[1]
    me = lax.axis_index("tp")
    total = None
    for ref in hidden:
        one = ref[:, depth : depth + LANES].astype(f32) + ref[:, depth + LANES :].astype(f32)
        total = one if total is None else total + one
    norm = lax.rsqrt(total / WIDTH + norm_eps)
    norm = jnp.concatenate([norm] * (wide // LANES), axis=1)
    copies = []
    for i, weight in enumerate(weights):
        cols = pl.ds(i * wide, wide)
        value = near_ref[:, cols]
        for k in range(1, parts):
            owner = lax.rem(me + parts - k, parts)
            rows = pl.ds(pl.multiple_of(owner * depth, LANES), depth)
            value = value + jnp.dot(
                hidden[k][:, :depth], weight[rows], preferred_element_type=f32
            )
        out_ref[:, cols] = (value * norm).astype(bf16)
        copy = pltpu.make_async_copy(out_ref.at[:, cols], out_hbm.at[:, cols], sems.at[i])
        copy.start()
        copies.append(copy)
    for copy in copies:
        copy.wait()


def on_device(queries, key_rows, value_rows, gate_input, norm_gain, doc_ids, out_weight):
    rows, width = queries.shape
    features = out_weight.shape[1]
    blocks, parts = lax.axis_size("seq"), lax.axis_size("tp")
    units = width // UC
    group = units * SPLITS
    back = -(-(-(-(DOC_MOST - 1) // rows)) // group)
    matchings = [(s, odd) for s in range(1, back + 1) for odd in range(2) if (odd + 1) * s * group < blocks]
    ids = doc_ids.reshape(1, rows)
    gain = norm_gain.reshape(1, WIDTH)
    dma = pltpu.SemaphoreType.DMA
    block16 = pltpu.VMEM((rows, width), bf16)
    ids_block = pltpu.VMEM((1, rows), jnp.int32)
    packet = jax.ShapeDtypeStruct((PACKET, LANES), bf16)
    body = jax.ShapeDtypeStruct((BODY, LANES), bf16)
    wide = jax.ShapeDtypeStruct((rows, width), f32)
    third = pltpu.VMEM((out_weight.shape[0], features // 3), bf16)

    def swap(value, pairs):
        return lax.ppermute(value, "seq", pairs)

    def trade(values):
        return [values[0]] + [
            swap(values[k], [(i, i ^ k) for i in range(blocks)]) for k in range(1, group)
        ]

    def matching(shift, odd):
        step = shift * group
        lower = [i for i in range(blocks - step) if (i // step) % 2 == odd]
        return [(i, i + step) for i in lower] + [(i + step, i) for i in lower]

    def load(index, after):
        return call(
            functools.partial(load_kernel, index),
            [third],
            (after, out_weight),
            "weight_load",
            scratch=[dma((LOADS,))],
            far_in=(1,),
            moved=2 * out_weight.size * 2 // 3,
        )[0]

    own = call(
        functools.partial(own_kernel, group),
        [packet] * group,
        (key_rows, value_rows, ids),
        "own_states",
        scratch=[block16, block16, ids_block, dma((1 + 2 * units,))],
        far_in=(0, 1, 2),
    )
    packets = trade(own)
    intra, scale, opened, weight0 = call(
        intra_kernel,
        [wide, wide, jax.ShapeDtypeStruct((rows, width), bf16), third],
        (own[0], queries, key_rows, value_rows, gate_input, gain, ids, out_weight),
        "intra",
        scratch=[block16] * 4 + [pltpu.VMEM((1, WIDTH), f32), ids_block, dma((6,)), dma((LOADS,))],
        far_in=range(1, 8),
        flops=4 * rows * rows * UNIT * width,
        moved=2 * out_weight.size * 2 // 3,
    )
    (summed,) = call(
        functools.partial(group_kernel, group), [packet], (intra, *packets), "group_state"
    )
    earlier = [swap(summed, matching(s, odd)) for s, odd in matchings]
    weight1 = load(1, summed)
    prefixes = call(
        functools.partial(prefix_kernel, group, matchings),
        [body] * group,
        (weight1, *packets, *earlier),
        "prefix_states",
        scratch=[pltpu.VMEM((group * PACKET, LANES), bf16), pltpu.VMEM((group * BODY, LANES), bf16)],
    )
    states = trade(prefixes)
    weight2 = load(2, prefixes[0])
    (hidden,) = call(
        functools.partial(hidden_kernel, group),
        [jax.ShapeDtypeStruct((rows, width + 2 * LANES), bf16)],
        (opened, intra, scale, weight2, *states),
        "hidden",
        scratch=[pltpu.VMEM((group * BODY, LANES), bf16)],
    )
    others = [
        lax.ppermute(hidden, "tp", [(i, (i + k) % parts) for i in range(parts)])
        for k in range(1, parts)
    ]
    weights = (weight0, weight1, weight2)
    (near,) = call(
        near_kernel,
        [jax.ShapeDtypeStruct((rows, features), f32)],
        (hidden, *weights),
        "near",
        flops=2 * rows * width * features,
        moved=2 * width * features,
    )
    (out,) = call(
        functools.partial(far_kernel, parts),
        [jax.ShapeDtypeStruct((rows, features), bf16)],
        (near, *weights, hidden, *others),
        "far",
        scratch=[pltpu.VMEM((rows, features), bf16), dma((3,))],
        far_out=(0,),
        flops=2 * rows * width * features,
        moved=2 * width * features,
    )
    return out


def solution(mesh):
    return jax.shard_map(
        on_device,
        mesh=mesh,
        in_specs=(
            P("seq", "tp"),
            P("seq", "tp"),
            P("seq", "tp"),
            P("seq", "tp"),
            P(),
            P("seq"),
            P(None, "tp"),
        ),
        out_specs=P("seq", "tp"),
        check_vma=False,
    )
```

```python
import functools

import jax
import jax.numpy as jnp
from jax import lax
from jax.experimental import pallas as pl
from jax.experimental.pallas import tpu as pltpu
from jax.sharding import PartitionSpec as P

HEADS = 32
HD = 96
WIDTH = HEADS * HD
DOC_MOST = 1024
UNIT = 4
UC = UNIT * HD
LANES = 128
BODY = HD * (UC // LANES)
IDS = 16
PACKET = BODY + IDS
LOADS = 4
norm_eps = 1e-05

bf16 = jnp.bfloat16
f32 = jnp.float32
IN_VMEM = pl.BlockSpec(memory_space=pltpu.VMEM)
IN_HBM = pl.BlockSpec(memory_space=pltpu.HBM)


def call(kernel, outs, args, name, limit=16, scratch=(), far_in=(), far_out=(), flops=0, moved=0):
    args = [
        pltpu.with_memory_space_constraint(arg, pltpu.HBM) if i in far_in else arg
        for i, arg in enumerate(args)
    ]
    return pl.pallas_call(
        kernel,
        out_shape=outs,
        in_specs=[IN_HBM if i in far_in else IN_VMEM for i in range(len(args))],
        out_specs=[IN_HBM if i in far_out else IN_VMEM for i in range(len(outs))],
        scratch_shapes=list(scratch),
        compiler_params=pltpu.CompilerParams(vmem_limit_bytes=limit << 20),
        cost_estimate=pl.CostEstimate(flops=flops, bytes_accessed=moved, transcendentals=0),
        name=name,
    )(*args)


def fetch(pairs, sems):
    copies = [pltpu.make_async_copy(src, dst, sems.at[i]) for i, (src, dst) in enumerate(pairs)]
    for copy in copies:
        copy.start()
    return copies


def lane_head(shape):
    return lax.broadcasted_iota(jnp.int32, shape, 1) // HD


def diagonal(blocks, head):
    total = blocks[0]
    for a in range(1, UNIT):
        total = jnp.where(head == a, blocks[a], total)
    return total


def id_column(ids):
    rows = ids.shape[1]
    return jnp.broadcast_to(ids, (rows, rows)).T


def orders(group):
    near = sorted(range(group), key=lambda k: (k > 0, -k.bit_count(), k))
    far = sorted(range(group), key=lambda k: (k > 0, -k.bit_count(), -k))
    return near, far


def helpers(group):
    place = lax.rem(lax.axis_index("seq"), group)
    even = lax.rem(lax.axis_index("tp"), 2) == 0
    return place, [place ^ jnp.where(even, a, b) for a, b in zip(*orders(group))]


def rows_of(index, size):
    return pl.ds(pl.multiple_of(index * size, 16), size)


def own_kernel(group, key_hbm, value_hbm, doc_hbm, *refs):
    packets, (key_ref, value_ref, doc_ref, sems) = refs[:group], refs[group:]
    columns = []
    pairs = [(doc_hbm, doc_ref)]
    for unit in helpers(group)[1]:
        cols = pl.ds(pl.multiple_of(unit * UC, LANES), UC)
        columns.append(cols)
        pairs += [(key_hbm.at[:, cols], key_ref.at[:, cols])]
        pairs += [(value_hbm.at[:, cols], value_ref.at[:, cols])]
    copies = fetch(pairs, sems)
    copies[0].wait()
    ids = doc_ref[...].astype(f32)
    first = jnp.min(ids, axis=1, keepdims=True)
    last = jnp.max(ids, axis=1, keepdims=True)
    keep = id_column(ids) == last
    keep = jnp.concatenate([keep] * (UC // keep.shape[1]), axis=1)
    head = lane_head((HD, UC))
    marks = jnp.where(
        lax.broadcasted_iota(jnp.int32, (IDS, LANES), 0) < IDS // 2,
        jnp.broadcast_to(last, (IDS, LANES)),
        jnp.broadcast_to(first, (IDS, LANES)),
    ).astype(bf16)
    for i, cols in enumerate(columns):
        copies[2 * i + 1].wait()
        copies[2 * i + 2].wait()
        keys = jnp.where(keep, key_ref[:, cols], jnp.zeros((), bf16))
        full = lax.dot_general(
            keys, value_ref[:, cols], (((0,), (0,)), ((), ())), preferred_element_type=f32
        )
        state = diagonal([full[a * HD : (a + 1) * HD] for a in range(UNIT)], head).astype(bf16)
        for c in range(UC // LANES):
            packets[i][c * HD : (c + 1) * HD] = state[:, c * LANES : (c + 1) * LANES]
        packets[i][BODY:] = marks


def read_packet(ref, base=0):
    marks = ref[base + BODY : base + PACKET].astype(f32)
    return ref[base : base + BODY].astype(f32), marks[0:1], marks[IDS // 2 : IDS // 2 + 1]


def group_kernel(group, beside_ref, *refs):
    packets, out_ref = [read_packet(ref) for ref in refs[:group]], refs[group]
    last = functools.reduce(jnp.maximum, [item[1] for item in packets])
    total = jnp.zeros((BODY, LANES), f32)
    for state, now, _ in packets:
        total = total + jnp.where(now == last, state, 0.0)
    out_ref[:BODY] = total.astype(bf16)
    out_ref[BODY:] = jnp.broadcast_to(last, (IDS, LANES)).astype(bf16)


def prefix_kernel(group, matchings, beside_ref, *refs):
    count = group + len(matchings)
    packets, earlier = refs[:group], refs[group:count]
    outs, (in_order, done) = refs[count:-2], refs[-2:]
    places = helpers(group)[1]
    own_group = lax.axis_index("seq") // group
    for place, packet in zip(places, packets):
        in_order[rows_of(place, PACKET)] = packet[...]
    own, last, first = read_packet(in_order)
    before = jnp.zeros((BODY, LANES), f32)
    for ref, (shift, odd) in zip(earlier, matchings):
        second = lax.rem(own_group // shift, 2) == 1 - odd
        valid = jnp.where(second & (own_group >= shift), 1.0, 0.0)
        state, now, _ = read_packet(ref)
        before = before + jnp.where(now == first, valid, 0.0) * state
    for j in range(group):
        if j:
            before_last = last
            through = own + jnp.where(last == first, before, 0.0)
            own, last, first = read_packet(in_order, j * PACKET)
            before = jnp.where(before_last == first, through, 0.0)
        done[j * BODY : (j + 1) * BODY] = before.astype(bf16)
    for place, out in zip(places, outs):
        out[...] = done[rows_of(place, BODY)]


def start_load(weight_hbm, third, out_ref, sems):
    rows, columns = out_ref.shape
    step = rows // LOADS
    return fetch(
        [
            (
                weight_hbm.at[pl.ds(i * step, step), pl.ds(third * columns, columns)],
                out_ref.at[pl.ds(i * step, step)],
            )
            for i in range(LOADS)
        ],
        sems,
    )


def load_kernel(third, after_ref, weight_hbm, out_ref, sems):
    for copy in start_load(weight_hbm, third, out_ref, sems):
        copy.wait()


def intra_kernel(
    after_ref, query_hbm, key_hbm, value_hbm, gate_hbm, gain_hbm, doc_hbm, weight_hbm,
    intra_ref, scale_ref, open_ref, weight_ref,
    query_ref, key_ref, value_ref, gate_ref, gain_ref, doc_ref, sems, load_sems,
):
    rows, width = query_ref.shape
    copies = fetch(
        [
            (doc_hbm, doc_ref),
            (query_hbm, query_ref),
            (key_hbm, key_ref),
            (value_hbm, value_ref),
            (gain_hbm, gain_ref),
            (gate_hbm, gate_ref),
        ],
        sems,
    )
    loads = start_load(weight_hbm, 0, weight_ref, load_sems)
    copies[0].wait()
    ids = doc_ref[...].astype(f32)
    column = id_column(ids)
    causal = lax.broadcasted_iota(jnp.int32, (rows, rows), 0) >= lax.broadcasted_iota(
        jnp.int32, (rows, rows), 1
    )
    keep = jnp.concatenate([(column == ids) & causal] * UNIT, axis=0)
    opened = column == jnp.min(ids, axis=1, keepdims=True)
    opened = jnp.concatenate([opened] * (UC // rows), axis=1)
    head = lane_head((rows, UC))
    part = lax.axis_index("tp")
    for copy in copies[1:4]:
        copy.wait()
    for u in range(width // UC):
        cols = slice(u * UC, (u + 1) * UC)
        query = query_ref[:, cols]
        open_ref[:, cols] = jnp.where(opened, query, jnp.zeros((), bf16))
        stacked = jnp.concatenate(
            [jnp.where(head == a, query, jnp.zeros((), bf16)) for a in range(UNIT)], axis=0
        )
        scores = lax.dot_general(
            stacked, key_ref[:, cols], (((1,), (1,)), ((), ())), preferred_element_type=f32
        )
        scores = jnp.where(keep, scores, 0.0).astype(bf16)
        mixed = jnp.dot(scores, value_ref[:, cols], preferred_element_type=f32)
        intra_ref[:, cols] = diagonal(
            [mixed[a * rows : (a + 1) * rows] for a in range(UNIT)], head
        )
    copies[4].wait()
    copies[5].wait()
    for u in range(width // UC):
        cols = slice(u * UC, (u + 1) * UC)
        gain = gain_ref[:, pl.ds(pl.multiple_of(part * width + u * UC, LANES), UC)]
        scale_ref[:, cols] = gain * jax.nn.sigmoid(gate_ref[:, cols].astype(f32))
    for load in loads:
        load.wait()


def hidden_kernel(group, open_ref, intra_ref, scale_ref, beside_ref, *refs):
    states, (out_ref, in_order) = refs[:group], refs[group:]
    rows, width = open_ref.shape
    for place, state in zip(helpers(group)[1], states):
        in_order[rows_of(place, BODY)] = state[...]
    head = lane_head((HD, UC))
    squares = jnp.zeros((rows, LANES), f32)
    for u in range(width // UC):
        cols = slice(u * UC, (u + 1) * UC)
        state = jnp.concatenate(
            [
                in_order[u * BODY + c * HD : u * BODY + (c + 1) * HD]
                for c in range(UC // LANES)
            ],
            axis=1,
        )
        spread = jnp.concatenate(
            [jnp.where(head == a, state, jnp.zeros((), bf16)) for a in range(UNIT)], axis=0
        )
        carried = jnp.dot(open_ref[:, cols], spread, preferred_element_type=f32)
        attn = (intra_ref[:, cols] + carried).astype(bf16).astype(f32)
        power = attn * attn
        for c in range(UC // LANES):
            squares = squares + power[:, c * LANES : (c + 1) * LANES]
        out_ref[:, cols] = (attn * scale_ref[:, cols]).astype(bf16)
    total = jnp.broadcast_to(jnp.sum(squares, axis=1, keepdims=True), (rows, LANES))
    high = total.astype(bf16)
    out_ref[:, width : width + LANES] = high
    out_ref[:, width + LANES :] = (total - high.astype(f32)).astype(bf16)


def near_kernel(hidden_ref, *refs):
    *weights, out_ref = refs
    depth = hidden_ref.shape[1] - 2 * LANES
    rows = pl.ds(pl.multiple_of(lax.axis_index("tp") * depth, LANES), depth)
    wide = weights[0].shape[1]
    for i, weight in enumerate(weights):
        out_ref[:, i * wide : (i + 1) * wide] = jnp.dot(
            hidden_ref[:, :depth], weight[rows], preferred_element_type=f32
        )


def far_kernel(parts, near_ref, *refs):
    weights, hidden, (out_hbm, out_ref, sems) = refs[:3], refs[3:-3], refs[-3:]
    depth = hidden[0].shape[1] - 2 * LANES
    wide = weights[0].shape[1]
    me = lax.axis_index("tp")
    total = None
    for ref in hidden:
        one = ref[:, depth : depth + LANES].astype(f32) + ref[:, depth + LANES :].astype(f32)
        total = one if total is None else total + one
    norm = lax.rsqrt(total / WIDTH + norm_eps)
    norm = jnp.concatenate([norm] * (wide // 2 // LANES), axis=1)
    copies = []
    half = wide // 2
    for i in range(2 * len(weights)):
        weight, inner = weights[i // 2], pl.ds(i % 2 * half, half)
        cols = pl.ds(i * half, half)
        value = near_ref[:, cols]
        for k in range(1, parts):
            owner = lax.rem(me + parts - k, parts)
            rows = pl.ds(pl.multiple_of(owner * depth, LANES), depth)
            value = value + jnp.dot(
                hidden[k][:, :depth], weight[rows, inner], preferred_element_type=f32
            )
        out_ref[:, cols] = (value * norm).astype(bf16)
        copy = pltpu.make_async_copy(out_ref.at[:, cols], out_hbm.at[:, cols], sems.at[i])
        copy.start()
        copies.append(copy)
    for copy in copies:
        copy.wait()


def on_device(queries, key_rows, value_rows, gate_input, norm_gain, doc_ids, out_weight):
    rows, width = queries.shape
    features = out_weight.shape[1]
    blocks, parts = lax.axis_size("seq"), lax.axis_size("tp")
    units = width // UC
    group = units
    back = -(-(-(-(DOC_MOST - 1) // rows)) // group)
    matchings = [
        (s, odd)
        for s in range(1, back + 1)
        for odd in range(2)
        if (odd + 1) * s * group < blocks
    ]
    ids = doc_ids.reshape(1, rows)
    gain = norm_gain.reshape(1, WIDTH)
    dma = pltpu.SemaphoreType.DMA
    block16 = pltpu.VMEM((rows, width), bf16)
    ids_block = pltpu.VMEM((1, rows), jnp.int32)
    packet = jax.ShapeDtypeStruct((PACKET, LANES), bf16)
    body = jax.ShapeDtypeStruct((BODY, LANES), bf16)
    wide = jax.ShapeDtypeStruct((rows, width), f32)
    third = pltpu.VMEM((out_weight.shape[0], features // 3), bf16)

    def swap(value, partner):
        pairs = [
            (i * parts + t, partner(i, t) * parts + t) for i in range(blocks) for t in range(parts)
        ]
        return lax.ppermute(value, ("seq", "tp"), pairs)

    def trade(values):
        return [values[0]] + [
            swap(values[j], lambda i, t: i ^ orders(group)[t % 2][j]) for j in range(1, group)
        ]

    def matching(shift, odd):
        step = shift * group

        def partner(i, t):
            other = i + step if (i // step) % 2 == odd else i - step
            return other if 0 <= other < blocks else i

        return partner

    def load(index, after):
        return call(
            functools.partial(load_kernel, index),
            [third],
            (after, out_weight),
            "weight_load",
            scratch=[dma((LOADS,))],
            far_in=(1,),
            moved=2 * out_weight.size * 2 // 3,
        )[0]

    own = call(
        functools.partial(own_kernel, group),
        [packet] * group,
        (key_rows, value_rows, ids),
        "own_states",
        scratch=[block16, block16, ids_block, dma((1 + 2 * units,))],
        far_in=(0, 1, 2),
    )
    packets = trade(own)
    intra, scale, opened, weight0 = call(
        intra_kernel,
        [wide, wide, jax.ShapeDtypeStruct((rows, width), bf16), third],
        (own[0], queries, key_rows, value_rows, gate_input, gain, ids, out_weight),
        "intra",
        scratch=[block16] * 4 + [pltpu.VMEM((1, WIDTH), f32), ids_block, dma((6,)), dma((LOADS,))],
        far_in=range(1, 8),
        flops=4 * rows * rows * UNIT * width,
        moved=2 * out_weight.size * 2 // 3,
    )
    (summed,) = call(
        functools.partial(group_kernel, group), [packet], (intra, *packets), "group_state"
    )
    earlier = [swap(summed, matching(s, odd)) for s, odd in matchings]
    weight1 = load(1, summed)
    prefixes = call(
        functools.partial(prefix_kernel, group, matchings),
        [body] * group,
        (weight1, *packets, *earlier),
        "prefix_states",
        scratch=[pltpu.VMEM((group * PACKET, LANES), bf16), pltpu.VMEM((group * BODY, LANES), bf16)],
    )
    states = trade(prefixes)
    weight2 = load(2, prefixes[0])
    (hidden,) = call(
        functools.partial(hidden_kernel, group),
        [jax.ShapeDtypeStruct((rows, width + 2 * LANES), bf16)],
        (opened, intra, scale, weight2, *states),
        "hidden",
        scratch=[pltpu.VMEM((group * BODY, LANES), bf16)],
    )
    others = [
        lax.ppermute(hidden, "tp", [(i, (i + k) % parts) for i in range(parts)])
        for k in range(1, parts)
    ]
    weights = (weight0, weight1, weight2)
    (near,) = call(
        near_kernel,
        [jax.ShapeDtypeStruct((rows, features), f32)],
        (hidden, *weights),
        "near",
        flops=2 * rows * width * features,
        moved=2 * width * features,
    )
    (out,) = call(
        functools.partial(far_kernel, parts),
        [jax.ShapeDtypeStruct((rows, features), bf16)],
        (near, *weights, hidden, *others),
        "far",
        scratch=[pltpu.VMEM((rows, features), bf16), dma((6,))],
        far_out=(0,),
        flops=2 * rows * width * features,
        moved=2 * width * features,
    )
    return out


def solution(mesh):
    return jax.shard_map(
        on_device,
        mesh=mesh,
        in_specs=(
            P("seq", "tp"),
            P("seq", "tp"),
            P("seq", "tp"),
            P("seq", "tp"),
            P(),
            P("seq"),
            P(None, "tp"),
        ),
        out_specs=P("seq", "tp"),
        check_vma=False,
    )
```

```python
import functools

import jax
import jax.numpy as jnp
from jax import lax
from jax.experimental import pallas as pl
from jax.experimental.pallas import tpu as pltpu
from jax.sharding import PartitionSpec as P

HEADS = 32
HD = 96
WIDTH = HEADS * HD
DOC_MOST = 1024
UNIT = 4
UC = UNIT * HD
LANES = 128
BODY = HD * (UC // LANES)
IDS = 16
PACKET = BODY + IDS
LOADS = 8
norm_eps = 1e-05

bf16 = jnp.bfloat16
f32 = jnp.float32
IN_VMEM = pl.BlockSpec(memory_space=pltpu.VMEM)
IN_HBM = pl.BlockSpec(memory_space=pltpu.HBM)


def call(kernel, outs, args, name, limit=16, scratch=(), far_in=(), far_out=(), flops=0, moved=0):
    args = [
        pltpu.with_memory_space_constraint(arg, pltpu.HBM) if i in far_in else arg
        for i, arg in enumerate(args)
    ]
    return pl.pallas_call(
        kernel,
        out_shape=outs,
        in_specs=[IN_HBM if i in far_in else IN_VMEM for i in range(len(args))],
        out_specs=[IN_HBM if i in far_out else IN_VMEM for i in range(len(outs))],
        scratch_shapes=list(scratch),
        compiler_params=pltpu.CompilerParams(vmem_limit_bytes=limit << 20),
        cost_estimate=pl.CostEstimate(flops=flops, bytes_accessed=moved, transcendentals=0),
        name=name,
    )(*args)


def fetch(pairs, sems):
    copies = [pltpu.make_async_copy(src, dst, sems.at[i]) for i, (src, dst) in enumerate(pairs)]
    for copy in copies:
        copy.start()
    return copies


def lane_head(shape):
    return lax.broadcasted_iota(jnp.int32, shape, 1) // HD


def diagonal(blocks, head):
    total = blocks[0]
    for a in range(1, UNIT):
        total = jnp.where(head == a, blocks[a], total)
    return total


def id_column(ids):
    rows = ids.shape[1]
    return jnp.broadcast_to(ids, (rows, rows)).T


def orders(group):
    near = sorted(range(group), key=lambda k: (k > 0, -k.bit_count(), k))
    far = sorted(range(group), key=lambda k: (k > 0, -k.bit_count(), -k))
    return near, far


def helpers(group):
    place = lax.rem(lax.axis_index("seq"), group)
    even = lax.rem(lax.axis_index("tp"), 2) == 0
    return place, [place ^ jnp.where(even, a, b) for a, b in zip(*orders(group))]


def rows_of(index, size):
    return pl.ds(pl.multiple_of(index * size, 16), size)


def own_kernel(group, key_hbm, value_hbm, doc_hbm, *refs):
    packets, (key_ref, value_ref, doc_ref, sems) = refs[:group], refs[group:]
    columns = []
    pairs = [(doc_hbm, doc_ref)]
    for unit in helpers(group)[1]:
        cols = pl.ds(pl.multiple_of(unit * UC, LANES), UC)
        columns.append(cols)
        pairs += [(key_hbm.at[:, cols], key_ref.at[:, cols])]
        pairs += [(value_hbm.at[:, cols], value_ref.at[:, cols])]
    copies = fetch(pairs, sems)
    copies[0].wait()
    ids = doc_ref[...].astype(f32)
    first = jnp.min(ids, axis=1, keepdims=True)
    last = jnp.max(ids, axis=1, keepdims=True)
    keep = id_column(ids) == last
    keep = jnp.concatenate([keep] * (UC // keep.shape[1]), axis=1)
    head = lane_head((HD, UC))
    marks = jnp.where(
        lax.broadcasted_iota(jnp.int32, (IDS, LANES), 0) < IDS // 2,
        jnp.broadcast_to(last, (IDS, LANES)),
        jnp.broadcast_to(first, (IDS, LANES)),
    ).astype(bf16)
    for i, cols in enumerate(columns):
        copies[2 * i + 1].wait()
        copies[2 * i + 2].wait()
        keys = jnp.where(keep, key_ref[:, cols], jnp.zeros((), bf16))
        full = lax.dot_general(
            keys, value_ref[:, cols], (((0,), (0,)), ((), ())), preferred_element_type=f32
        )
        state = diagonal([full[a * HD : (a + 1) * HD] for a in range(UNIT)], head).astype(bf16)
        for c in range(UC // LANES):
            packets[i][c * HD : (c + 1) * HD] = state[:, c * LANES : (c + 1) * LANES]
        packets[i][BODY:] = marks


def read_packet(ref, base=0):
    marks = ref[base + BODY : base + PACKET].astype(f32)
    return ref[base : base + BODY].astype(f32), marks[0:1], marks[IDS // 2 : IDS // 2 + 1]


def group_kernel(group, beside_ref, *refs):
    packets, out_ref = [read_packet(ref) for ref in refs[:group]], refs[group]
    last = functools.reduce(jnp.maximum, [item[1] for item in packets])
    total = jnp.zeros((BODY, LANES), f32)
    for state, now, _ in packets:
        total = total + jnp.where(now == last, state, 0.0)
    out_ref[:BODY] = total.astype(bf16)
    out_ref[BODY:] = jnp.broadcast_to(last, (IDS, LANES)).astype(bf16)


def prefix_kernel(group, matchings, beside_ref, *refs):
    count = group + len(matchings)
    packets, earlier = refs[:group], refs[group:count]
    outs, (in_order, done) = refs[count:-2], refs[-2:]
    places = helpers(group)[1]
    own_group = lax.axis_index("seq") // group
    for place, packet in zip(places, packets):
        in_order[rows_of(place, PACKET)] = packet[...]
    own, last, first = read_packet(in_order)
    before = jnp.zeros((BODY, LANES), f32)
    for ref, (shift, odd) in zip(earlier, matchings):
        second = lax.rem(own_group // shift, 2) == 1 - odd
        valid = jnp.where(second & (own_group >= shift), 1.0, 0.0)
        state, now, _ = read_packet(ref)
        before = before + jnp.where(now == first, valid, 0.0) * state
    for j in range(group):
        if j:
            before_last = last
            through = own + jnp.where(last == first, before, 0.0)
            own, last, first = read_packet(in_order, j * PACKET)
            before = jnp.where(before_last == first, through, 0.0)
        done[j * BODY : (j + 1) * BODY] = before.astype(bf16)
    for place, out in zip(places, outs):
        out[...] = done[rows_of(place, BODY)]


def start_load(weight_hbm, third, out_ref, sems):
    rows, columns = out_ref.shape
    step = rows // LOADS
    return fetch(
        [
            (
                weight_hbm.at[pl.ds(i * step, step), pl.ds(third * columns, columns)],
                out_ref.at[pl.ds(i * step, step)],
            )
            for i in range(LOADS)
        ],
        sems,
    )


def gate_kernel(
    after_ref, gate_hbm, gain_hbm, weight_hbm,
    scale_ref, weight_ref,
    gate_ref, gain_ref, sems, load_sems,
):
    width = gate_ref.shape[1]
    copies = fetch([(gate_hbm, gate_ref), (gain_hbm, gain_ref)], sems)
    loads = start_load(weight_hbm, 1, weight_ref, load_sems)
    part = lax.axis_index("tp")
    for copy in copies:
        copy.wait()
    for u in range(width // UC):
        cols = slice(u * UC, (u + 1) * UC)
        gain = gain_ref[:, pl.ds(pl.multiple_of(part * width + u * UC, LANES), UC)]
        scale_ref[:, cols] = gain * jax.nn.sigmoid(gate_ref[:, cols].astype(f32))
    for load in loads:
        load.wait()


def load_kernel(after_ref, weight_hbm, out_ref, sems):
    for copy in start_load(weight_hbm, 2, out_ref, sems):
        copy.wait()


def intra_kernel(
    after_ref, key_ref, value_ref, query_hbm, doc_hbm, weight_hbm,
    intra_ref, open_ref, weight_ref,
    query_ref, doc_ref, sems, load_sems,
):
    rows, width = query_ref.shape
    copies = fetch([(doc_hbm, doc_ref), (query_hbm, query_ref)], sems)
    loads = start_load(weight_hbm, 0, weight_ref, load_sems)
    copies[0].wait()
    ids = doc_ref[...].astype(f32)
    column = id_column(ids)
    causal = lax.broadcasted_iota(jnp.int32, (rows, rows), 0) >= lax.broadcasted_iota(
        jnp.int32, (rows, rows), 1
    )
    keep = jnp.concatenate([(column == ids) & causal] * UNIT, axis=0)
    opened = column == jnp.min(ids, axis=1, keepdims=True)
    opened = jnp.concatenate([opened] * (UC // rows), axis=1)
    head = lane_head((rows, UC))
    copies[1].wait()
    for u in range(width // UC):
        cols = slice(u * UC, (u + 1) * UC)
        query = query_ref[:, cols]
        open_ref[:, cols] = jnp.where(opened, query, jnp.zeros((), bf16))
        stacked = jnp.concatenate(
            [jnp.where(head == a, query, jnp.zeros((), bf16)) for a in range(UNIT)], axis=0
        )
        scores = lax.dot_general(
            stacked, key_ref[:, cols], (((1,), (1,)), ((), ())), preferred_element_type=f32
        )
        scores = jnp.where(keep, scores, 0.0).astype(bf16)
        mixed = jnp.dot(scores, value_ref[:, cols], preferred_element_type=f32)
        intra_ref[:, cols] = diagonal(
            [mixed[a * rows : (a + 1) * rows] for a in range(UNIT)], head
        )
    for load in loads:
        load.wait()


def hidden_kernel(group, open_ref, intra_ref, scale_ref, beside_ref, *refs):
    states, (out_ref, in_order) = refs[:group], refs[group:]
    rows, width = open_ref.shape
    for place, state in zip(helpers(group)[1], states):
        in_order[rows_of(place, BODY)] = state[...]
    head = lane_head((HD, UC))
    squares = jnp.zeros((rows, LANES), f32)
    for u in range(width // UC):
        cols = slice(u * UC, (u + 1) * UC)
        state = jnp.concatenate(
            [
                in_order[u * BODY + c * HD : u * BODY + (c + 1) * HD]
                for c in range(UC // LANES)
            ],
            axis=1,
        )
        spread = jnp.concatenate(
            [jnp.where(head == a, state, jnp.zeros((), bf16)) for a in range(UNIT)], axis=0
        )
        carried = jnp.dot(open_ref[:, cols], spread, preferred_element_type=f32)
        attn = (intra_ref[:, cols] + carried).astype(bf16).astype(f32)
        power = attn * attn
        for c in range(UC // LANES):
            squares = squares + power[:, c * LANES : (c + 1) * LANES]
        out_ref[:, cols] = (attn * scale_ref[:, cols]).astype(bf16)
    total = jnp.broadcast_to(jnp.sum(squares, axis=1, keepdims=True), (rows, LANES))
    high = total.astype(bf16)
    out_ref[:, width : width + LANES] = high
    out_ref[:, width + LANES :] = (total - high.astype(f32)).astype(bf16)


def near_kernel(hidden_ref, *refs):
    *weights, out_ref = refs
    depth = hidden_ref.shape[1] - 2 * LANES
    rows = pl.ds(pl.multiple_of(lax.axis_index("tp") * depth, LANES), depth)
    wide = weights[0].shape[1]
    for i, weight in enumerate(weights):
        out_ref[:, i * wide : (i + 1) * wide] = jnp.dot(
            hidden_ref[:, :depth], weight[rows], preferred_element_type=f32
        )


def far_kernel(parts, near_ref, *refs):
    weights, hidden, (out_hbm, out_ref, sems) = refs[:3], refs[3:-3], refs[-3:]
    depth = hidden[0].shape[1] - 2 * LANES
    step = out_ref.shape[1] // 6
    me = lax.axis_index("tp")
    total = None
    for ref in hidden:
        one = ref[:, depth : depth + LANES].astype(f32) + ref[:, depth + LANES :].astype(f32)
        total = one if total is None else total + one
    norm = lax.rsqrt(total / WIDTH + norm_eps)
    norm = jnp.concatenate([norm] * (step // LANES), axis=1)
    copies = []
    pieces = [(w, c) for w in weights for c in range(0, w.shape[1], step)]
    for i, (weight, column) in enumerate(pieces):
        inner, cols = pl.ds(column, step), pl.ds(i * step, step)
        value = near_ref[:, cols]
        for k in range(1, parts):
            owner = lax.rem(me + parts - k, parts)
            rows = pl.ds(pl.multiple_of(owner * depth, LANES), depth)
            value = value + jnp.dot(
                hidden[k][:, :depth], weight[rows, inner], preferred_element_type=f32
            )
        out_ref[:, cols] = (value * norm).astype(bf16)
        copy = pltpu.make_async_copy(out_ref.at[:, cols], out_hbm.at[:, cols], sems.at[i])
        copy.start()
        copies.append(copy)
    for copy in copies:
        copy.wait()


def on_device(queries, key_rows, value_rows, gate_input, norm_gain, doc_ids, out_weight):
    rows, width = queries.shape
    features = out_weight.shape[1]
    blocks, parts = lax.axis_size("seq"), lax.axis_size("tp")
    units = width // UC
    group = units
    back = -(-(-(-(DOC_MOST - 1) // rows)) // group)
    matchings = [
        (s, odd)
        for odd in (0, 1)
        for s in range(1, back + 1)
        if (odd + 1) * s * group < blocks
    ]
    ids = doc_ids.reshape(1, rows)
    gain = norm_gain.reshape(1, WIDTH)
    dma = pltpu.SemaphoreType.DMA
    ids_block = pltpu.VMEM((1, rows), jnp.int32)
    packet = jax.ShapeDtypeStruct((PACKET, LANES), bf16)
    body = jax.ShapeDtypeStruct((BODY, LANES), bf16)
    wide = jax.ShapeDtypeStruct((rows, width), f32)
    narrow = jax.ShapeDtypeStruct((rows, width), bf16)
    third = pltpu.VMEM((out_weight.shape[0], features // 3), bf16)
    moved = 4 * out_weight.size // 3

    def swap(value, partner):
        pairs = [
            (i * parts + t, partner(i, t) * parts + t) for i in range(blocks) for t in range(parts)
        ]
        return lax.ppermute(value, ("seq", "tp"), pairs)

    def trade(values):
        return [values[0]] + [
            swap(values[j], lambda i, t: i ^ orders(group)[t % 2][j]) for j in range(1, group)
        ]

    def matching(shift, odd):
        step = shift * group

        def partner(i, t):
            other = i + step if (i // step) % 2 == odd else i - step
            return other if 0 <= other < blocks else i

        return partner

    *own, key_block, value_block = call(
        functools.partial(own_kernel, group),
        [packet] * group + [narrow] * 2,
        (key_rows, value_rows, ids),
        "own_states",
        scratch=[ids_block, dma((1 + 2 * units,))],
        far_in=(0, 1, 2),
    )
    packets = trade(own)
    intra, opened, weight0 = call(
        intra_kernel,
        [wide, narrow, third],
        (own[0], key_block, value_block, queries, ids, out_weight),
        "intra",
        scratch=[pltpu.VMEM((rows, width), bf16), ids_block, dma((2,)), dma((LOADS,))],
        far_in=(3, 4, 5),
        flops=4 * rows * rows * UNIT * width,
        moved=moved,
    )
    (summed,) = call(
        functools.partial(group_kernel, group), [packet], (intra, *packets), "group_state"
    )
    earlier = [swap(summed, matching(s, odd)) for s, odd in matchings]
    scale, weight1 = call(
        gate_kernel,
        [wide, third],
        (summed, gate_input, gain, out_weight),
        "gate",
        scratch=[
            pltpu.VMEM((rows, width), bf16),
            pltpu.VMEM((1, WIDTH), f32),
            dma((2,)),
            dma((LOADS,)),
        ],
        far_in=(1, 2, 3),
        moved=moved,
    )
    prefixes = call(
        functools.partial(prefix_kernel, group, matchings),
        [body] * group,
        (weight1, *packets, *earlier),
        "prefix_states",
        scratch=[pltpu.VMEM((group * PACKET, LANES), bf16), pltpu.VMEM((group * BODY, LANES), bf16)],
    )
    states = trade(prefixes)
    (weight2,) = call(
        load_kernel,
        [third],
        (prefixes[0], out_weight),
        "weight_load",
        scratch=[dma((LOADS,))],
        far_in=(1,),
        moved=moved,
    )
    (hidden,) = call(
        functools.partial(hidden_kernel, group),
        [jax.ShapeDtypeStruct((rows, width + 2 * LANES), bf16)],
        (opened, intra, scale, weight2, *states),
        "hidden",
        scratch=[pltpu.VMEM((group * BODY, LANES), bf16)],
    )
    others = [
        lax.ppermute(hidden, "tp", [(i, (i + k) % parts) for i in range(parts)])
        for k in range(1, parts)
    ]
    (near,) = call(
        near_kernel,
        [jax.ShapeDtypeStruct((rows, features), f32)],
        (hidden, weight0, weight1, weight2),
        "near",
        flops=2 * rows * width * features,
        moved=2 * width * features,
    )
    (out,) = call(
        functools.partial(far_kernel, parts),
        [jax.ShapeDtypeStruct((rows, features), bf16)],
        (near, weight0, weight1, weight2, hidden, *others),
        "far",
        scratch=[pltpu.VMEM((rows, features), bf16), dma((6,))],
        far_out=(0,),
        flops=2 * rows * width * features,
        moved=2 * width * features,
    )
    return out


def solution(mesh):
    return jax.shard_map(
        on_device,
        mesh=mesh,
        in_specs=(
            P("seq", "tp"),
            P("seq", "tp"),
            P("seq", "tp"),
            P("seq", "tp"),
            P(),
            P("seq"),
            P(None, "tp"),
        ),
        out_specs=P("seq", "tp"),
        check_vma=False,
    )
```

```python
import functools

import jax
import jax.numpy as jnp
from jax import lax
from jax.experimental import pallas as pl
from jax.experimental.pallas import tpu as pltpu
from jax.sharding import PartitionSpec as P

HEADS = 32
HD = 96
WIDTH = HEADS * HD
DOC_MOST = 1024
UNIT = 4
UC = UNIT * HD
LANES = 128
BODY = HD * (UC // LANES)
IDS = 16
PACKET = BODY + IDS
LOADS = 4
norm_eps = 1e-05

bf16 = jnp.bfloat16
f32 = jnp.float32
IN_VMEM = pl.BlockSpec(memory_space=pltpu.VMEM)
IN_HBM = pl.BlockSpec(memory_space=pltpu.HBM)


def call(kernel, outs, args, name, limit=16, scratch=(), far_in=(), far_out=(), flops=0, moved=0):
    args = [
        pltpu.with_memory_space_constraint(arg, pltpu.HBM) if i in far_in else arg
        for i, arg in enumerate(args)
    ]
    return pl.pallas_call(
        kernel,
        out_shape=outs,
        in_specs=[IN_HBM if i in far_in else IN_VMEM for i in range(len(args))],
        out_specs=[IN_HBM if i in far_out else IN_VMEM for i in range(len(outs))],
        scratch_shapes=list(scratch),
        compiler_params=pltpu.CompilerParams(vmem_limit_bytes=limit << 20),
        cost_estimate=pl.CostEstimate(flops=flops, bytes_accessed=moved, transcendentals=0),
        name=name,
    )(*args)


def fetch(pairs, sems):
    copies = [pltpu.make_async_copy(src, dst, sems.at[i]) for i, (src, dst) in enumerate(pairs)]
    for copy in copies:
        copy.start()
    return copies


def lane_head(shape):
    return lax.broadcasted_iota(jnp.int32, shape, 1) // HD


def diagonal(blocks, head):
    total = blocks[0]
    for a in range(1, UNIT):
        total = jnp.where(head == a, blocks[a], total)
    return total


def id_column(ids):
    rows = ids.shape[1]
    return jnp.broadcast_to(ids, (rows, rows)).T


def orders(group):
    near = sorted(range(group), key=lambda k: (k > 0, -k.bit_count(), k))
    far = sorted(range(group), key=lambda k: (k > 0, -k.bit_count(), -k))
    return near, far


def helpers(group):
    place = lax.rem(lax.axis_index("seq"), group)
    even = lax.rem(lax.axis_index("tp"), 2) == 0
    return place, [place ^ jnp.where(even, a, b) for a, b in zip(*orders(group))]


def rows_of(index, size):
    return pl.ds(pl.multiple_of(index * size, 16), size)


def own_kernel(group, key_hbm, value_hbm, doc_hbm, *refs):
    packets, (key_ref, value_ref, doc_ref, sems) = refs[:group], refs[group:]
    columns = []
    pairs = [(doc_hbm, doc_ref)]
    for unit in helpers(group)[1]:
        cols = pl.ds(pl.multiple_of(unit * UC, LANES), UC)
        columns.append(cols)
        pairs += [(key_hbm.at[:, cols], key_ref.at[:, cols])]
        pairs += [(value_hbm.at[:, cols], value_ref.at[:, cols])]
    copies = fetch(pairs, sems)
    copies[0].wait()
    ids = doc_ref[...].astype(f32)
    first = jnp.min(ids, axis=1, keepdims=True)
    last = jnp.max(ids, axis=1, keepdims=True)
    keep = id_column(ids) == last
    keep = jnp.concatenate([keep] * (UC // keep.shape[1]), axis=1)
    head = lane_head((HD, UC))
    marks = jnp.where(
        lax.broadcasted_iota(jnp.int32, (IDS, LANES), 0) < IDS // 2,
        jnp.broadcast_to(last, (IDS, LANES)),
        jnp.broadcast_to(first, (IDS, LANES)),
    ).astype(bf16)
    for i, cols in enumerate(columns):
        copies[2 * i + 1].wait()
        copies[2 * i + 2].wait()
        keys = jnp.where(keep, key_ref[:, cols], jnp.zeros((), bf16))
        full = lax.dot_general(
            keys, value_ref[:, cols], (((0,), (0,)), ((), ())), preferred_element_type=f32
        )
        state = diagonal([full[a * HD : (a + 1) * HD] for a in range(UNIT)], head).astype(bf16)
        for c in range(UC // LANES):
            packets[i][c * HD : (c + 1) * HD] = state[:, c * LANES : (c + 1) * LANES]
        packets[i][BODY:] = marks


def read_packet(ref, base=0):
    marks = ref[base + BODY : base + PACKET].astype(f32)
    return ref[base : base + BODY].astype(f32), marks[0:1], marks[IDS // 2 : IDS // 2 + 1]


def group_kernel(group, beside_ref, *refs):
    packets, out_ref = [read_packet(ref) for ref in refs[:group]], refs[group]
    last = functools.reduce(jnp.maximum, [item[1] for item in packets])
    total = jnp.zeros((BODY, LANES), f32)
    for state, now, _ in packets:
        total = total + jnp.where(now == last, state, 0.0)
    out_ref[:BODY] = total.astype(bf16)
    out_ref[BODY:] = jnp.broadcast_to(last, (IDS, LANES)).astype(bf16)


def prefix_kernel(group, matchings, beside_ref, *refs):
    count = group + len(matchings)
    packets, earlier = refs[:group], refs[group:count]
    outs, (in_order, done) = refs[count:-2], refs[-2:]
    places = helpers(group)[1]
    own_group = lax.axis_index("seq") // group
    for place, packet in zip(places, packets):
        in_order[rows_of(place, PACKET)] = packet[...]
    own, last, first = read_packet(in_order)
    before = jnp.zeros((BODY, LANES), f32)
    for ref, (shift, odd) in zip(earlier, matchings):
        second = lax.rem(own_group // shift, 2) == 1 - odd
        valid = jnp.where(second & (own_group >= shift), 1.0, 0.0)
        state, now, _ = read_packet(ref)
        before = before + jnp.where(now == first, valid, 0.0) * state
    for j in range(group):
        if j:
            before_last = last
            through = own + jnp.where(last == first, before, 0.0)
            own, last, first = read_packet(in_order, j * PACKET)
            before = jnp.where(before_last == first, through, 0.0)
        done[j * BODY : (j + 1) * BODY] = before.astype(bf16)
    for place, out in zip(places, outs):
        out[...] = done[rows_of(place, BODY)]


def start_load(weight_hbm, third, out_ref, sems):
    rows, columns = out_ref.shape
    step = rows // LOADS
    return fetch(
        [
            (
                weight_hbm.at[pl.ds(i * step, step), pl.ds(third * columns, columns)],
                out_ref.at[pl.ds(i * step, step)],
            )
            for i in range(LOADS)
        ],
        sems,
    )


def gate_kernel(
    after_ref, gate_hbm, gain_hbm, weight_hbm,
    scale_ref, weight_ref,
    gate_ref, gain_ref, sems, load_sems,
):
    width = gate_ref.shape[1]
    copies = fetch([(gate_hbm, gate_ref), (gain_hbm, gain_ref)], sems)
    loads = start_load(weight_hbm, 1, weight_ref, load_sems)
    part = lax.axis_index("tp")
    for copy in copies:
        copy.wait()
    for u in range(width // UC):
        cols = slice(u * UC, (u + 1) * UC)
        gain = gain_ref[:, pl.ds(pl.multiple_of(part * width + u * UC, LANES), UC)]
        scale_ref[:, cols] = gain * jax.nn.sigmoid(gate_ref[:, cols].astype(f32))
    for load in loads:
        load.wait()


def load_kernel(after_ref, weight_hbm, out_ref, sems):
    for copy in start_load(weight_hbm, 2, out_ref, sems):
        copy.wait()


def intra_kernel(
    after_ref, key_ref, value_ref, query_hbm, doc_hbm, weight_hbm,
    intra_ref, open_ref, weight_ref,
    query_ref, doc_ref, sems, load_sems,
):
    rows, width = query_ref.shape
    units = [pl.ds(u * UC, UC) for u in range(width // UC)]
    copies = fetch(
        [(doc_hbm, doc_ref)] + [(query_hbm.at[:, c], query_ref.at[:, c]) for c in units], sems
    )
    loads = start_load(weight_hbm, 0, weight_ref, load_sems)
    copies[0].wait()
    ids = doc_ref[...].astype(f32)
    column = id_column(ids)
    causal = lax.broadcasted_iota(jnp.int32, (rows, rows), 0) >= lax.broadcasted_iota(
        jnp.int32, (rows, rows), 1
    )
    keep = jnp.concatenate([(column == ids) & causal] * UNIT, axis=0)
    opened = column == jnp.min(ids, axis=1, keepdims=True)
    opened = jnp.concatenate([opened] * (UC // rows), axis=1)
    head = lane_head((rows, UC))
    for cols, copy in zip(units, copies[1:]):
        copy.wait()
        query = query_ref[:, cols]
        open_ref[:, cols] = jnp.where(opened, query, jnp.zeros((), bf16))
        stacked = jnp.concatenate(
            [jnp.where(head == a, query, jnp.zeros((), bf16)) for a in range(UNIT)], axis=0
        )
        scores = lax.dot_general(
            stacked, key_ref[:, cols], (((1,), (1,)), ((), ())), preferred_element_type=f32
        )
        scores = jnp.where(keep, scores, 0.0).astype(bf16)
        mixed = jnp.dot(scores, value_ref[:, cols], preferred_element_type=f32)
        intra_ref[:, cols] = diagonal(
            [mixed[a * rows : (a + 1) * rows] for a in range(UNIT)], head
        )
    for load in loads:
        load.wait()


def hidden_kernel(group, open_ref, intra_ref, scale_ref, beside_ref, *refs):
    states, (out_ref, in_order) = refs[:group], refs[group:]
    rows, width = open_ref.shape
    for place, state in zip(helpers(group)[1], states):
        in_order[rows_of(place, BODY)] = state[...]
    head = lane_head((HD, UC))
    squares = jnp.zeros((rows, LANES), f32)
    for u in range(width // UC):
        cols = slice(u * UC, (u + 1) * UC)
        state = jnp.concatenate(
            [
                in_order[u * BODY + c * HD : u * BODY + (c + 1) * HD]
                for c in range(UC // LANES)
            ],
            axis=1,
        )
        spread = jnp.concatenate(
            [jnp.where(head == a, state, jnp.zeros((), bf16)) for a in range(UNIT)], axis=0
        )
        carried = jnp.dot(open_ref[:, cols], spread, preferred_element_type=f32)
        attn = (intra_ref[:, cols] + carried).astype(bf16).astype(f32)
        power = attn * attn
        for c in range(UC // LANES):
            squares = squares + power[:, c * LANES : (c + 1) * LANES]
        out_ref[:, cols] = (attn * scale_ref[:, cols]).astype(bf16)
    total = jnp.broadcast_to(jnp.sum(squares, axis=1, keepdims=True), (rows, LANES))
    high = total.astype(bf16)
    low = (total - high.astype(f32)).astype(bf16)
    lane = lax.broadcasted_iota(jnp.int32, (rows, LANES), 1)
    out_ref[:, width:] = jnp.where(lane < LANES // 2, high, low)


def near_kernel(hidden_ref, *refs):
    *weights, out_ref = refs
    depth = hidden_ref.shape[1] - LANES
    rows = pl.ds(pl.multiple_of(lax.axis_index("tp") * depth, LANES), depth)
    wide = weights[0].shape[1]
    for i, weight in enumerate(weights):
        out_ref[:, i * wide : (i + 1) * wide] = jnp.dot(
            hidden_ref[:, :depth], weight[rows], preferred_element_type=f32
        )


def far_kernel(parts, near_ref, *refs):
    weights, hidden, (out_hbm, out_ref, sems) = refs[:3], refs[3:-3], refs[-3:]
    depth = hidden[0].shape[1] - LANES
    step = out_ref.shape[1] // 6
    me = lax.axis_index("tp")
    total = None
    for ref in hidden:
        one = ref[:, depth:].astype(f32)
        one = one + pltpu.roll(one, LANES // 2, 1)
        total = one if total is None else total + one
    norm = lax.rsqrt(total / WIDTH + norm_eps)
    norm = jnp.concatenate([norm] * (step // LANES), axis=1)
    copies = []
    pieces = [(w, c) for w in weights for c in range(0, w.shape[1], step)]
    for i, (weight, column) in enumerate(pieces):
        inner, cols = pl.ds(column, step), pl.ds(i * step, step)
        value = near_ref[:, cols]
        for k in range(1, parts):
            owner = lax.rem(me + parts - k, parts)
            rows = pl.ds(pl.multiple_of(owner * depth, LANES), depth)
            value = value + jnp.dot(
                hidden[k][:, :depth], weight[rows, inner], preferred_element_type=f32
            )
        out_ref[:, cols] = (value * norm).astype(bf16)
        copy = pltpu.make_async_copy(out_ref.at[:, cols], out_hbm.at[:, cols], sems.at[i])
        copy.start()
        copies.append(copy)
    for copy in copies:
        copy.wait()


def on_device(queries, key_rows, value_rows, gate_input, norm_gain, doc_ids, out_weight):
    rows, width = queries.shape
    features = out_weight.shape[1]
    blocks, parts = lax.axis_size("seq"), lax.axis_size("tp")
    units = width // UC
    group = units
    back = -(-(-(-(DOC_MOST - 1) // rows)) // group)
    matchings = [
        (s, odd)
        for odd in (1, 0)
        for s in range(back, 0, -1)
        if (odd + 1) * s * group < blocks
    ]
    ids = doc_ids.reshape(1, rows)
    gain = norm_gain.reshape(1, WIDTH)
    dma = pltpu.SemaphoreType.DMA
    ids_block = pltpu.VMEM((1, rows), jnp.int32)
    packet = jax.ShapeDtypeStruct((PACKET, LANES), bf16)
    body = jax.ShapeDtypeStruct((BODY, LANES), bf16)
    wide = jax.ShapeDtypeStruct((rows, width), f32)
    narrow = jax.ShapeDtypeStruct((rows, width), bf16)
    third = pltpu.VMEM((out_weight.shape[0], features // 3), bf16)
    moved = 4 * out_weight.size // 3

    def swap(value, partner):
        pairs = [
            (i * parts + t, partner(i, t) * parts + t) for i in range(blocks) for t in range(parts)
        ]
        return lax.ppermute(value, ("seq", "tp"), pairs)

    def trade(values):
        return [values[0]] + [
            swap(values[j], lambda i, t: i ^ orders(group)[t % 2][j]) for j in range(1, group)
        ]

    def matching(shift, odd):
        step = shift * group

        def partner(i, t):
            other = i + step if (i // step) % 2 == odd else i - step
            return other if 0 <= other < blocks else i

        return partner

    *own, key_block, value_block = call(
        functools.partial(own_kernel, group),
        [packet] * group + [narrow] * 2,
        (key_rows, value_rows, ids),
        "own_states",
        scratch=[ids_block, dma((1 + 2 * units,))],
        far_in=(0, 1, 2),
    )
    packets = trade(own)
    intra, opened, weight0 = call(
        intra_kernel,
        [wide, narrow, third],
        (own[0], key_block, value_block, queries, ids, out_weight),
        "intra",
        scratch=[pltpu.VMEM((rows, width), bf16), ids_block, dma((1 + units,)), dma((LOADS,))],
        far_in=(3, 4, 5),
        flops=4 * rows * rows * UNIT * width,
        moved=moved,
    )
    (summed,) = call(
        functools.partial(group_kernel, group), [packet], (intra, *packets), "group_state"
    )
    earlier = [swap(summed, matching(s, odd)) for s, odd in matchings]
    scale, weight1 = call(
        gate_kernel,
        [wide, third],
        (summed, gate_input, gain, out_weight),
        "gate",
        scratch=[
            pltpu.VMEM((rows, width), bf16),
            pltpu.VMEM((1, WIDTH), f32),
            dma((2,)),
            dma((LOADS,)),
        ],
        far_in=(1, 2, 3),
        moved=moved,
    )
    prefixes = call(
        functools.partial(prefix_kernel, group, matchings),
        [body] * group,
        (weight1, *packets, *earlier),
        "prefix_states",
        scratch=[pltpu.VMEM((group * PACKET, LANES), bf16), pltpu.VMEM((group * BODY, LANES), bf16)],
    )
    states = trade(prefixes)
    (weight2,) = call(
        load_kernel,
        [third],
        (prefixes[0], out_weight),
        "weight_load",
        scratch=[dma((LOADS,))],
        far_in=(1,),
        moved=moved,
    )
    (hidden,) = call(
        functools.partial(hidden_kernel, group),
        [jax.ShapeDtypeStruct((rows, width + LANES), bf16)],
        (opened, intra, scale, weight2, *states),
        "hidden",
        scratch=[pltpu.VMEM((group * BODY, LANES), bf16)],
    )
    others = [
        lax.ppermute(hidden, "tp", [(i, (i + k) % parts) for i in range(parts)])
        for k in range(1, parts)
    ]
    (near,) = call(
        near_kernel,
        [jax.ShapeDtypeStruct((rows, features), f32)],
        (hidden, weight0, weight1, weight2),
        "near",
        flops=2 * rows * width * features,
        moved=2 * width * features,
    )
    (out,) = call(
        functools.partial(far_kernel, parts),
        [jax.ShapeDtypeStruct((rows, features), bf16)],
        (near, weight0, weight1, weight2, hidden, *others),
        "far",
        scratch=[pltpu.VMEM((rows, features), bf16), dma((6,))],
        far_out=(0,),
        flops=2 * rows * width * features,
        moved=2 * width * features,
    )
    return out


def solution(mesh):
    return jax.shard_map(
        on_device,
        mesh=mesh,
        in_specs=(
            P("seq", "tp"),
            P("seq", "tp"),
            P("seq", "tp"),
            P("seq", "tp"),
            P(),
            P("seq"),
            P(None, "tp"),
        ),
        out_specs=P("seq", "tp"),
        check_vma=False,
    )
```

```python
import functools

import jax
import jax.numpy as jnp
from jax import lax
from jax.experimental import pallas as pl
from jax.experimental.pallas import tpu as pltpu
from jax.sharding import PartitionSpec as P

HEADS = 32
HD = 96
WIDTH = HEADS * HD
DOC_MOST = 1024
UNIT = 4
UC = UNIT * HD
LANES = 128
BODY = HD * (UC // LANES)
IDS = 16
PACKET = BODY + IDS
LOADS = 4
norm_eps = 1e-05

bf16 = jnp.bfloat16
f32 = jnp.float32
IN_VMEM = pl.BlockSpec(memory_space=pltpu.VMEM)
IN_HBM = pl.BlockSpec(memory_space=pltpu.HBM)


def call(kernel, outs, args, name, limit=16, scratch=(), far_in=(), far_out=(), flops=0, moved=0):
    args = [
        pltpu.with_memory_space_constraint(arg, pltpu.HBM) if i in far_in else arg
        for i, arg in enumerate(args)
    ]
    return pl.pallas_call(
        kernel,
        out_shape=outs,
        in_specs=[IN_HBM if i in far_in else IN_VMEM for i in range(len(args))],
        out_specs=[IN_HBM if i in far_out else IN_VMEM for i in range(len(outs))],
        scratch_shapes=list(scratch),
        compiler_params=pltpu.CompilerParams(vmem_limit_bytes=limit << 20),
        cost_estimate=pl.CostEstimate(flops=flops, bytes_accessed=moved, transcendentals=0),
        name=name,
    )(*args)


def fetch(pairs, sems):
    copies = [pltpu.make_async_copy(src, dst, sems.at[i]) for i, (src, dst) in enumerate(pairs)]
    for copy in copies:
        copy.start()
    return copies


def lane_head(shape):
    return lax.broadcasted_iota(jnp.int32, shape, 1) // HD


def diagonal(blocks, head):
    total = blocks[0]
    for a in range(1, UNIT):
        total = jnp.where(head == a, blocks[a], total)
    return total


def id_column(ids):
    rows = ids.shape[1]
    return jnp.broadcast_to(ids, (rows, rows)).T


def orders(group):
    near = sorted(range(group), key=lambda k: (k > 0, -k.bit_count(), k))
    far = sorted(range(group), key=lambda k: (k > 0, -k.bit_count(), -k))
    return near, far


def helpers(group):
    place = lax.rem(lax.axis_index("seq"), group)
    even = lax.rem(lax.axis_index("tp"), 2) == 0
    return place, [place ^ jnp.where(even, a, b) for a, b in zip(*orders(group))]


def rows_of(index, size):
    return pl.ds(pl.multiple_of(index * size, 16), size)


def own_kernel(group, key_hbm, value_hbm, doc_hbm, *refs):
    packets, (key_ref, value_ref, doc_ref, sems) = refs[:group], refs[group:]
    columns = []
    pairs = [(doc_hbm, doc_ref)]
    for unit in helpers(group)[1]:
        cols = pl.ds(pl.multiple_of(unit * UC, LANES), UC)
        columns.append((unit, cols))
        pairs += [(key_hbm.at[:, cols], key_ref.at[:, cols])]
        pairs += [(value_hbm.at[:, cols], value_ref.at[:, cols])]
    copies = fetch(pairs, sems)
    copies[0].wait()
    ids = doc_ref[...].astype(f32)
    first = jnp.min(ids, axis=1, keepdims=True)
    last = jnp.max(ids, axis=1, keepdims=True)
    keep = jnp.where(ids == last, 1.0, 0.0).astype(bf16)
    lane = lax.broadcasted_iota(jnp.int32, (HD, LANES), 1)
    marks = jnp.where(
        lax.broadcasted_iota(jnp.int32, (IDS, LANES), 0) < IDS // 2,
        jnp.broadcast_to(last, (IDS, LANES)),
        jnp.broadcast_to(first, (IDS, LANES)),
    ).astype(bf16)
    for i, (unit, cols) in enumerate(columns):
        copies[2 * i + 1].wait()
        copies[2 * i + 2].wait()
        turned = key_ref[:, cols].T * keep
        for c in range(UC // LANES):
            tile = pl.ds(pl.multiple_of(unit * UC + c * LANES, LANES), LANES)
            full = jnp.dot(
                turned[c * HD : (c + 2) * HD], value_ref[:, tile], preferred_element_type=f32
            )
            state = jnp.where(lane < HD - c * (LANES - HD), full[:HD], full[HD:])
            packets[i][c * HD : (c + 1) * HD] = state.astype(bf16)
        packets[i][BODY:] = marks


def read_packet(ref, base=0):
    marks = ref[base + BODY : base + PACKET].astype(f32)
    return ref[base : base + BODY].astype(f32), marks[0:1], marks[IDS // 2 : IDS // 2 + 1]


def group_kernel(group, beside_ref, *refs):
    packets, out_ref = [read_packet(ref) for ref in refs[:group]], refs[group]
    last = functools.reduce(jnp.maximum, [item[1] for item in packets])
    total = jnp.zeros((BODY, LANES), f32)
    for state, now, _ in packets:
        total = total + jnp.where(now == last, state, 0.0)
    out_ref[:BODY] = total.astype(bf16)
    out_ref[BODY:] = jnp.broadcast_to(last, (IDS, LANES)).astype(bf16)


def prefix_kernel(group, matchings, beside_ref, *refs):
    count = group + len(matchings)
    packets, earlier = refs[:group], refs[group:count]
    outs, (in_order, done) = refs[count:-2], refs[-2:]
    places = helpers(group)[1]
    own_group = lax.axis_index("seq") // group
    for place, packet in zip(places, packets):
        in_order[rows_of(place, PACKET)] = packet[...]
    own, last, first = read_packet(in_order)
    before = jnp.zeros((BODY, LANES), f32)
    for ref, (shift, odd) in zip(earlier, matchings):
        second = lax.rem(own_group // shift, 2) == 1 - odd
        valid = jnp.where(second & (own_group >= shift), 1.0, 0.0)
        state, now, _ = read_packet(ref)
        before = before + jnp.where(now == first, valid, 0.0) * state
    for j in range(group):
        if j:
            before_last = last
            through = own + jnp.where(last == first, before, 0.0)
            own, last, first = read_packet(in_order, j * PACKET)
            before = jnp.where(before_last == first, through, 0.0)
        done[j * BODY : (j + 1) * BODY] = before.astype(bf16)
    for place, out in zip(places, outs):
        out[...] = done[rows_of(place, BODY)]


def start_load(weight_hbm, third, out_ref, sems):
    rows, columns = out_ref.shape
    step = rows // LOADS
    return fetch(
        [
            (
                weight_hbm.at[pl.ds(i * step, step), pl.ds(third * columns, columns)],
                out_ref.at[pl.ds(i * step, step)],
            )
            for i in range(LOADS)
        ],
        sems,
    )


def gate_kernel(
    after_ref, gate_hbm, gain_hbm, weight_hbm,
    scale_ref, weight_ref,
    gate_ref, gain_ref, sems, load_sems,
):
    width = gate_ref.shape[1]
    copies = fetch([(gate_hbm, gate_ref), (gain_hbm, gain_ref)], sems)
    loads = start_load(weight_hbm, 1, weight_ref, load_sems)
    part = lax.axis_index("tp")
    for copy in copies:
        copy.wait()
    for u in range(width // UC):
        cols = slice(u * UC, (u + 1) * UC)
        gain = gain_ref[:, pl.ds(pl.multiple_of(part * width + u * UC, LANES), UC)]
        scale_ref[:, cols] = gain * jax.nn.sigmoid(gate_ref[:, cols].astype(f32))
    for load in loads:
        load.wait()


def load_kernel(after_ref, weight_hbm, out_ref, sems):
    for copy in start_load(weight_hbm, 2, out_ref, sems):
        copy.wait()


def intra_kernel(
    after_ref, key_ref, value_ref, query_hbm, doc_hbm, weight_hbm,
    intra_ref, open_ref, weight_ref,
    query_ref, doc_ref, sems, load_sems,
):
    rows, width = query_ref.shape
    units = [pl.ds(u * UC, UC) for u in range(width // UC)]
    copies = fetch(
        [(doc_hbm, doc_ref)] + [(query_hbm.at[:, c], query_ref.at[:, c]) for c in units], sems
    )
    loads = start_load(weight_hbm, 0, weight_ref, load_sems)
    copies[0].wait()
    ids = doc_ref[...].astype(f32)
    column = id_column(ids)
    causal = lax.broadcasted_iota(jnp.int32, (rows, rows), 0) >= lax.broadcasted_iota(
        jnp.int32, (rows, rows), 1
    )
    keep = jnp.concatenate([(column == ids) & causal] * UNIT, axis=0)
    opened = column == jnp.min(ids, axis=1, keepdims=True)
    opened = jnp.concatenate([opened] * (UC // rows), axis=1)
    head = lane_head((rows, UC))
    for cols, copy in zip(units, copies[1:]):
        copy.wait()
        query = query_ref[:, cols]
        open_ref[:, cols] = jnp.where(opened, query, jnp.zeros((), bf16))
        stacked = jnp.concatenate(
            [jnp.where(head == a, query, jnp.zeros((), bf16)) for a in range(UNIT)], axis=0
        )
        scores = lax.dot_general(
            stacked, key_ref[:, cols], (((1,), (1,)), ((), ())), preferred_element_type=f32
        )
        scores = jnp.where(keep, scores, 0.0).astype(bf16)
        mixed = jnp.dot(scores, value_ref[:, cols], preferred_element_type=f32)
        intra_ref[:, cols] = diagonal(
            [mixed[a * rows : (a + 1) * rows] for a in range(UNIT)], head
        )
    for load in loads:
        load.wait()


def hidden_kernel(group, open_ref, intra_ref, scale_ref, beside_ref, *refs):
    states, (out_ref, in_order) = refs[:group], refs[group:]
    rows, width = open_ref.shape
    for place, state in zip(helpers(group)[1], states):
        in_order[rows_of(place, BODY)] = state[...]
    head = lane_head((HD, UC))
    squares = jnp.zeros((rows, LANES), f32)
    for u in range(width // UC):
        cols = slice(u * UC, (u + 1) * UC)
        state = jnp.concatenate(
            [
                in_order[u * BODY + c * HD : u * BODY + (c + 1) * HD]
                for c in range(UC // LANES)
            ],
            axis=1,
        )
        spread = jnp.concatenate(
            [jnp.where(head == a, state, jnp.zeros((), bf16)) for a in range(UNIT)], axis=0
        )
        carried = jnp.dot(open_ref[:, cols], spread, preferred_element_type=f32)
        attn = (intra_ref[:, cols] + carried).astype(bf16).astype(f32)
        power = attn * attn
        for c in range(UC // LANES):
            squares = squares + power[:, c * LANES : (c + 1) * LANES]
        out_ref[:, cols] = (attn * scale_ref[:, cols]).astype(bf16)
    total = jnp.broadcast_to(jnp.sum(squares, axis=1, keepdims=True), (rows, LANES))
    high = total.astype(bf16)
    low = (total - high.astype(f32)).astype(bf16)
    lane = lax.broadcasted_iota(jnp.int32, (rows, LANES), 1)
    out_ref[:, width:] = jnp.where(lane < LANES // 2, high, low)


def near_kernel(hidden_ref, *refs):
    *weights, out_ref = refs
    depth = hidden_ref.shape[1] - LANES
    rows = pl.ds(pl.multiple_of(lax.axis_index("tp") * depth, LANES), depth)
    wide = weights[0].shape[1]
    for i, weight in enumerate(weights):
        out_ref[:, i * wide : (i + 1) * wide] = jnp.dot(
            hidden_ref[:, :depth], weight[rows], preferred_element_type=f32
        )


def far_kernel(parts, near_ref, *refs):
    weights, hidden, (out_hbm, out_ref, sems) = refs[:3], refs[3:-3], refs[-3:]
    depth = hidden[0].shape[1] - LANES
    step = out_ref.shape[1] // 6
    me = lax.axis_index("tp")
    total = None
    for ref in hidden:
        one = ref[:, depth:].astype(f32)
        one = one + pltpu.roll(one, LANES // 2, 1)
        total = one if total is None else total + one
    norm = lax.rsqrt(total / WIDTH + norm_eps)
    norm = jnp.concatenate([norm] * (step // LANES), axis=1)
    copies = []
    pieces = [(w, c) for w in weights for c in range(0, w.shape[1], step)]
    for i, (weight, column) in enumerate(pieces):
        inner, cols = pl.ds(column, step), pl.ds(i * step, step)
        value = near_ref[:, cols]
        for k in range(1, parts):
            owner = lax.rem(me + parts - k, parts)
            rows = pl.ds(pl.multiple_of(owner * depth, LANES), depth)
            value = value + jnp.dot(
                hidden[k][:, :depth], weight[rows, inner], preferred_element_type=f32
            )
        out_ref[:, cols] = (value * norm).astype(bf16)
        copy = pltpu.make_async_copy(out_ref.at[:, cols], out_hbm.at[:, cols], sems.at[i])
        copy.start()
        copies.append(copy)
    for copy in copies:
        copy.wait()


def on_device(queries, key_rows, value_rows, gate_input, norm_gain, doc_ids, out_weight):
    rows, width = queries.shape
    features = out_weight.shape[1]
    blocks, parts = lax.axis_size("seq"), lax.axis_size("tp")
    units = width // UC
    group = units
    back = -(-(-(-(DOC_MOST - 1) // rows)) // group)
    matchings = [
        (s, odd)
        for odd in (1, 0)
        for s in range(back, 0, -1)
        if (odd + 1) * s * group < blocks
    ]
    ids = doc_ids.reshape(1, rows)
    gain = norm_gain.reshape(1, WIDTH)
    dma = pltpu.SemaphoreType.DMA
    ids_block = pltpu.VMEM((1, rows), jnp.int32)
    packet = jax.ShapeDtypeStruct((PACKET, LANES), bf16)
    body = jax.ShapeDtypeStruct((BODY, LANES), bf16)
    wide = jax.ShapeDtypeStruct((rows, width), f32)
    narrow = jax.ShapeDtypeStruct((rows, width), bf16)
    third = pltpu.VMEM((out_weight.shape[0], features // 3), bf16)
    moved = 4 * out_weight.size // 3

    def swap(value, partner):
        pairs = [
            (i * parts + t, partner(i, t) * parts + t) for i in range(blocks) for t in range(parts)
        ]
        return lax.ppermute(value, ("seq", "tp"), pairs)

    def trade(values):
        return [values[0]] + [
            swap(values[j], lambda i, t: i ^ orders(group)[t % 2][j]) for j in range(1, group)
        ]

    def matching(shift, odd):
        step = shift * group

        def partner(i, t):
            other = i + step if (i // step) % 2 == odd else i - step
            return other if 0 <= other < blocks else i

        return partner

    *own, key_block, value_block = call(
        functools.partial(own_kernel, group),
        [packet] * group + [narrow] * 2,
        (key_rows, value_rows, ids),
        "own_states",
        scratch=[ids_block, dma((1 + 2 * units,))],
        far_in=(0, 1, 2),
    )
    packets = trade(own)
    intra, opened, weight0 = call(
        intra_kernel,
        [wide, narrow, third],
        (own[0], key_block, value_block, queries, ids, out_weight),
        "intra",
        scratch=[pltpu.VMEM((rows, width), bf16), ids_block, dma((1 + units,)), dma((LOADS,))],
        far_in=(3, 4, 5),
        flops=4 * rows * rows * UNIT * width,
        moved=moved,
    )
    (summed,) = call(
        functools.partial(group_kernel, group), [packet], (intra, *packets), "group_state"
    )
    earlier = [swap(summed, matching(s, odd)) for s, odd in matchings]
    scale, weight1 = call(
        gate_kernel,
        [wide, third],
        (summed, gate_input, gain, out_weight),
        "gate",
        scratch=[
            pltpu.VMEM((rows, width), bf16),
            pltpu.VMEM((1, WIDTH), f32),
            dma((2,)),
            dma((LOADS,)),
        ],
        far_in=(1, 2, 3),
        moved=moved,
    )
    prefixes = call(
        functools.partial(prefix_kernel, group, matchings),
        [body] * group,
        (weight1, *packets, *earlier),
        "prefix_states",
        scratch=[pltpu.VMEM((group * PACKET, LANES), bf16), pltpu.VMEM((group * BODY, LANES), bf16)],
    )
    states = trade(prefixes)
    (weight2,) = call(
        load_kernel,
        [third],
        (prefixes[0], out_weight),
        "weight_load",
        scratch=[dma((LOADS,))],
        far_in=(1,),
        moved=moved,
    )
    (hidden,) = call(
        functools.partial(hidden_kernel, group),
        [jax.ShapeDtypeStruct((rows, width + LANES), bf16)],
        (opened, intra, scale, weight2, *states),
        "hidden",
        scratch=[pltpu.VMEM((group * BODY, LANES), bf16)],
    )
    others = [
        lax.ppermute(hidden, "tp", [(i, (i + k) % parts) for i in range(parts)])
        for k in range(1, parts)
    ]
    (near,) = call(
        near_kernel,
        [jax.ShapeDtypeStruct((rows, features), f32)],
        (hidden, weight0, weight1, weight2),
        "near",
        flops=2 * rows * width * features,
        moved=2 * width * features,
    )
    (out,) = call(
        functools.partial(far_kernel, parts),
        [jax.ShapeDtypeStruct((rows, features), bf16)],
        (near, weight0, weight1, weight2, hidden, *others),
        "far",
        scratch=[pltpu.VMEM((rows, features), bf16), dma((6,))],
        far_out=(0,),
        flops=2 * rows * width * features,
        moved=2 * width * features,
    )
    return out


def solution(mesh):
    return jax.shard_map(
        on_device,
        mesh=mesh,
        in_specs=(
            P("seq", "tp"),
            P("seq", "tp"),
            P("seq", "tp"),
            P("seq", "tp"),
            P(),
            P("seq"),
            P(None, "tp"),
        ),
        out_specs=P("seq", "tp"),
        check_vma=False,
    )
```

```python
import functools
import math

import jax
import jax.numpy as jnp
from jax import lax
from jax.experimental import pallas as pl
from jax.experimental.pallas import tpu as pltpu
from jax.sharding import PartitionSpec as P

HEADS = 32
HD = 96
WIDTH = HEADS * HD
DOC_MOST = 1024
UNIT = 4
UC = UNIT * HD
LANES = 128
BODY = HD * (UC // LANES)
IDS = 16
PACKET = BODY + IDS
norm_eps = 1e-05

bf16 = jnp.bfloat16
f32 = jnp.float32
IN_VMEM = pl.BlockSpec(memory_space=pltpu.VMEM)
IN_HBM = pl.BlockSpec(memory_space=pltpu.HBM)


def call(kernel, outs, args, name, limit=16, scratch=(), far_in=(), far_out=(), flops=0, moved=0):
    args = [
        pltpu.with_memory_space_constraint(arg, pltpu.HBM) if i in far_in else arg
        for i, arg in enumerate(args)
    ]
    return pl.pallas_call(
        kernel,
        out_shape=outs,
        in_specs=[IN_HBM if i in far_in else IN_VMEM for i in range(len(args))],
        out_specs=[IN_HBM if i in far_out else IN_VMEM for i in range(len(outs))],
        scratch_shapes=list(scratch),
        compiler_params=pltpu.CompilerParams(vmem_limit_bytes=limit << 20),
        cost_estimate=pl.CostEstimate(flops=flops, bytes_accessed=moved, transcendentals=0),
        name=name,
    )(*args)


def fetch(pairs, sems):
    copies = [pltpu.make_async_copy(src, dst, sems.at[i]) for i, (src, dst) in enumerate(pairs)]
    for copy in copies:
        copy.start()
    return copies


def lane_head(shape):
    return lax.broadcasted_iota(jnp.int32, shape, 1) // HD


def diagonal(blocks, head):
    total = blocks[0]
    for a in range(1, UNIT):
        total = jnp.where(head == a, blocks[a], total)
    return total


def id_column(ids):
    rows = ids.shape[1]
    return jnp.broadcast_to(ids, (rows, rows)).T


def orders(group):
    near = sorted(range(group), key=lambda k: (k > 0, -k.bit_count(), k))
    far = sorted(range(group), key=lambda k: (k > 0, -k.bit_count(), -k))
    return near, far


def helpers(group):
    place = lax.rem(lax.axis_index("seq"), group)
    even = lax.rem(lax.axis_index("tp"), 2) == 0
    return place, [place ^ jnp.where(even, a, b) for a, b in zip(*orders(group))]


def rows_of(index, size):
    return pl.ds(pl.multiple_of(index * size, 16), size)


def own_kernel(group, key_hbm, value_hbm, doc_hbm, *refs):
    packets, (key_ref, value_ref, doc_ref, sems) = refs[:group], refs[group:]
    columns = []
    pairs = [(doc_hbm, doc_ref)]
    for unit in helpers(group)[1]:
        cols = pl.ds(pl.multiple_of(unit * UC, LANES), UC)
        columns.append((unit, cols))
        pairs += [(key_hbm.at[:, cols], key_ref.at[:, cols])]
        pairs += [(value_hbm.at[:, cols], value_ref.at[:, cols])]
    copies = fetch(pairs, sems)
    copies[0].wait()
    ids = doc_ref[...].astype(f32)
    first = jnp.min(ids, axis=1, keepdims=True)
    last = jnp.max(ids, axis=1, keepdims=True)
    keep = jnp.where(ids == last, 1.0, 0.0).astype(bf16)
    lane = lax.broadcasted_iota(jnp.int32, (HD, LANES), 1)
    marks = jnp.where(
        lax.broadcasted_iota(jnp.int32, (IDS, LANES), 0) < IDS // 2,
        jnp.broadcast_to(last, (IDS, LANES)),
        jnp.broadcast_to(first, (IDS, LANES)),
    ).astype(bf16)
    for i, (unit, cols) in enumerate(columns):
        copies[2 * i + 1].wait()
        copies[2 * i + 2].wait()
        turned = key_ref[:, cols].T * keep
        for c in range(UC // LANES):
            tile = pl.ds(pl.multiple_of(unit * UC + c * LANES, LANES), LANES)
            full = jnp.dot(
                turned[c * HD : (c + 2) * HD], value_ref[:, tile], preferred_element_type=f32
            )
            state = jnp.where(lane < HD - c * (LANES - HD), full[:HD], full[HD:])
            packets[i][c * HD : (c + 1) * HD] = state.astype(bf16)
        packets[i][BODY:] = marks


def read_packet(ref, base=0):
    marks = ref[base + BODY : base + PACKET].astype(f32)
    return ref[base : base + BODY].astype(f32), marks[0:1], marks[IDS // 2 : IDS // 2 + 1]


def group_kernel(group, beside_ref, *refs):
    packets, out_ref = [read_packet(ref) for ref in refs[:group]], refs[group]
    last = functools.reduce(jnp.maximum, [item[1] for item in packets])
    total = jnp.zeros((BODY, LANES), f32)
    for state, now, _ in packets:
        total = total + jnp.where(now == last, state, 0.0)
    out_ref[:BODY] = total.astype(bf16)
    out_ref[BODY:] = jnp.broadcast_to(last, (IDS, LANES)).astype(bf16)


def prefix_kernel(group, matchings, beside_ref, *refs):
    count = group + len(matchings)
    packets, earlier = refs[:group], refs[group:count]
    outs, (in_order, done) = refs[count:-2], refs[-2:]
    places = helpers(group)[1]
    own_group = lax.axis_index("seq") // group
    for place, packet in zip(places, packets):
        in_order[rows_of(place, PACKET)] = packet[...]
    own, last, first = read_packet(in_order)
    before = jnp.zeros((BODY, LANES), f32)
    for ref, (shift, odd) in zip(earlier, matchings):
        second = lax.rem(own_group // shift, 2) == 1 - odd
        valid = jnp.where(second & (own_group >= shift), 1.0, 0.0)
        state, now, _ = read_packet(ref)
        before = before + jnp.where(now == first, valid, 0.0) * state
    for j in range(group):
        if j:
            before_last = last
            through = own + jnp.where(last == first, before, 0.0)
            own, last, first = read_packet(in_order, j * PACKET)
            before = jnp.where(before_last == first, through, 0.0)
        done[j * BODY : (j + 1) * BODY] = before.astype(bf16)
    for place, out in zip(places, outs):
        out[...] = done[rows_of(place, BODY)]


def chunks_of(depth, rows):
    step = math.gcd(depth, rows // 3)
    return step, [
        (r // depth, r % depth, r // (rows // 3), r % (rows // 3)) for r in range(0, rows, step)
    ]


def start_load(weight_hbm, third, out_ref, sems, depth):
    rows, parts = weight_hbm.shape[0], weight_hbm.shape[0] // depth
    me = lax.axis_index("tp")
    step, chunks = chunks_of(depth, rows)
    pairs = []
    for part, offset, piece, start in chunks:
        if piece == third:
            owner = lax.rem(me + parts - part, parts)
            source = pl.ds(pl.multiple_of(owner * depth + offset, LANES), step)
            pairs.append((weight_hbm.at[source], out_ref.at[pl.ds(start, step)]))
    return fetch(pairs, sems)


def gate_kernel(
    after_ref, gate_hbm, gain_hbm, weight_hbm,
    scale_ref, weight_ref,
    gate_ref, gain_ref, sems, load_sems,
):
    width = gate_ref.shape[1]
    loads = start_load(weight_hbm, 1, weight_ref, load_sems, width)
    copies = fetch([(gate_hbm, gate_ref), (gain_hbm, gain_ref)], sems)
    part = lax.axis_index("tp")
    for copy in copies:
        copy.wait()
    for u in range(width // UC):
        cols = slice(u * UC, (u + 1) * UC)
        gain = gain_ref[:, pl.ds(pl.multiple_of(part * width + u * UC, LANES), UC)]
        scale_ref[:, cols] = gain * jax.nn.sigmoid(gate_ref[:, cols].astype(f32))
    for load in loads:
        load.wait()


def load_kernel(depth, after_ref, weight_hbm, out_ref, sems):
    for copy in start_load(weight_hbm, 2, out_ref, sems, depth):
        copy.wait()


def intra_kernel(
    after_ref, key_ref, value_ref, query_hbm, doc_hbm, weight_hbm,
    intra_ref, open_ref, weight_ref,
    query_ref, doc_ref, sems, load_sems,
):
    rows, width = query_ref.shape
    units = [pl.ds(u * UC, UC) for u in range(width // UC)]
    copies = fetch(
        [(doc_hbm, doc_ref)] + [(query_hbm.at[:, c], query_ref.at[:, c]) for c in units], sems
    )
    loads = start_load(weight_hbm, 0, weight_ref, load_sems, width)
    copies[0].wait()
    ids = doc_ref[...].astype(f32)
    column = id_column(ids)
    causal = lax.broadcasted_iota(jnp.int32, (rows, rows), 0) >= lax.broadcasted_iota(
        jnp.int32, (rows, rows), 1
    )
    keep = jnp.concatenate([(column == ids) & causal] * UNIT, axis=0)
    opened = column == jnp.min(ids, axis=1, keepdims=True)
    opened = jnp.concatenate([opened] * (UC // rows), axis=1)
    head = lane_head((rows, UC))
    for cols, copy in zip(units, copies[1:]):
        copy.wait()
        query = query_ref[:, cols]
        open_ref[:, cols] = jnp.where(opened, query, jnp.zeros((), bf16))
        stacked = jnp.concatenate(
            [jnp.where(head == a, query, jnp.zeros((), bf16)) for a in range(UNIT)], axis=0
        )
        scores = lax.dot_general(
            stacked, key_ref[:, cols], (((1,), (1,)), ((), ())), preferred_element_type=f32
        )
        scores = jnp.where(keep, scores, 0.0).astype(bf16)
        mixed = jnp.dot(scores, value_ref[:, cols], preferred_element_type=f32)
        intra_ref[:, cols] = diagonal(
            [mixed[a * rows : (a + 1) * rows] for a in range(UNIT)], head
        )
    for load in loads:
        load.wait()


def hidden_kernel(group, open_ref, intra_ref, scale_ref, beside_ref, *refs):
    states, out_ref = refs[:group], refs[group]
    rows, width = open_ref.shape
    head = lane_head((HD, UC))
    squares = jnp.zeros((rows, LANES), f32)
    for unit, state_ref in zip(helpers(group)[1], states):
        cols = pl.ds(pl.multiple_of(unit * UC, LANES), UC)
        state = jnp.concatenate(
            [state_ref[c * HD : (c + 1) * HD] for c in range(UC // LANES)], axis=1
        )
        spread = jnp.concatenate(
            [jnp.where(head == a, state, jnp.zeros((), bf16)) for a in range(UNIT)], axis=0
        )
        carried = jnp.dot(open_ref[:, cols], spread, preferred_element_type=f32)
        attn = (intra_ref[:, cols] + carried).astype(bf16).astype(f32)
        power = attn * attn
        for c in range(UC // LANES):
            squares = squares + power[:, c * LANES : (c + 1) * LANES]
        out_ref[:, cols] = (attn * scale_ref[:, cols]).astype(bf16)
    total = jnp.broadcast_to(jnp.sum(squares, axis=1, keepdims=True), (rows, LANES))
    high = total.astype(bf16)
    low = (total - high.astype(f32)).astype(bf16)
    lane = lax.broadcasted_iota(jnp.int32, (rows, LANES), 1)
    out_ref[:, width:] = jnp.where(lane < LANES // 2, high, low)


def product(hidden, weights, cols, parts):
    depth = hidden[0].shape[1] - LANES
    step, chunks = chunks_of(depth, 3 * weights[0].shape[0])
    total = None
    for part, offset, piece, start in chunks:
        if part in parts:
            one = jnp.dot(
                hidden[part][:, offset : offset + step],
                weights[piece][start : start + step, cols],
                preferred_element_type=f32,
            )
            total = one if total is None else total + one
    return total


def near_kernel(hidden_ref, *refs):
    *weights, out_ref = refs
    step = out_ref.shape[1] // 6
    for i in range(6):
        cols = pl.ds(i * step, step)
        out_ref[:, cols] = product([hidden_ref], weights, cols, (0,))


def far_kernel(parts, near_ref, *refs):
    weights, hidden, (out_hbm, out_ref, sems) = refs[:3], refs[3:-3], refs[-3:]
    depth = hidden[0].shape[1] - LANES
    step = out_ref.shape[1] // 6
    total = None
    for ref in hidden:
        one = ref[:, depth:].astype(f32)
        one = one + pltpu.roll(one, LANES // 2, 1)
        total = one if total is None else total + one
    norm = lax.rsqrt(total / WIDTH + norm_eps)
    norm = jnp.concatenate([norm] * (step // LANES), axis=1)
    copies = []
    for i in range(6):
        cols = pl.ds(i * step, step)
        value = near_ref[:, cols] + product(hidden, weights, cols, range(1, parts))
        out_ref[:, cols] = (value * norm).astype(bf16)
        copy = pltpu.make_async_copy(out_ref.at[:, cols], out_hbm.at[:, cols], sems.at[i])
        copy.start()
        copies.append(copy)
    for copy in copies:
        copy.wait()


def on_device(queries, key_rows, value_rows, gate_input, norm_gain, doc_ids, out_weight):
    rows, width = queries.shape
    features = out_weight.shape[1]
    blocks, parts = lax.axis_size("seq"), lax.axis_size("tp")
    units = width // UC
    group = units
    back = -(-(-(-(DOC_MOST - 1) // rows)) // group)
    matchings = [
        (s, odd)
        for odd in (1, 0)
        for s in range(back, 0, -1)
        if (odd + 1) * s * group < blocks
    ]
    ids = doc_ids.reshape(1, rows)
    gain = norm_gain.reshape(1, WIDTH)
    dma = pltpu.SemaphoreType.DMA
    ids_block = pltpu.VMEM((1, rows), jnp.int32)
    packet = jax.ShapeDtypeStruct((PACKET, LANES), bf16)
    body = jax.ShapeDtypeStruct((BODY, LANES), bf16)
    wide = jax.ShapeDtypeStruct((rows, width), f32)
    narrow = jax.ShapeDtypeStruct((rows, width), bf16)
    third = pltpu.VMEM((out_weight.shape[0] // 3, features), bf16)
    loads = out_weight.shape[0] // 3 // chunks_of(width, out_weight.shape[0])[0]
    moved = 4 * out_weight.size // 3

    def swap(value, partner):
        pairs = [
            (i * parts + t, partner(i, t) * parts + t) for i in range(blocks) for t in range(parts)
        ]
        return lax.ppermute(value, ("seq", "tp"), pairs)

    def trade(values):
        return [values[0]] + [
            swap(values[j], lambda i, t: i ^ orders(group)[t % 2][j]) for j in range(1, group)
        ]

    def matching(shift, odd):
        step = shift * group

        def partner(i, t):
            other = i + step if (i // step) % 2 == odd else i - step
            return other if 0 <= other < blocks else i

        return partner

    *own, key_block, value_block = call(
        functools.partial(own_kernel, group),
        [packet] * group + [narrow] * 2,
        (key_rows, value_rows, ids),
        "own_states",
        scratch=[ids_block, dma((1 + 2 * units,))],
        far_in=(0, 1, 2),
    )
    packets = trade(own)
    intra, opened, weight0 = call(
        intra_kernel,
        [wide, narrow, third],
        (own[0], key_block, value_block, queries, ids, out_weight),
        "intra",
        scratch=[pltpu.VMEM((rows, width), bf16), ids_block, dma((1 + units,)), dma((loads,))],
        far_in=(3, 4, 5),
        flops=4 * rows * rows * UNIT * width,
        moved=moved,
    )
    (summed,) = call(
        functools.partial(group_kernel, group), [packet], (intra, *packets), "group_state"
    )
    earlier = [swap(summed, matching(s, odd)) for s, odd in matchings]
    scale, weight1 = call(
        gate_kernel,
        [wide, third],
        (summed, gate_input, gain, out_weight),
        "gate",
        scratch=[
            pltpu.VMEM((rows, width), bf16),
            pltpu.VMEM((1, WIDTH), f32),
            dma((2,)),
            dma((loads,)),
        ],
        far_in=(1, 2, 3),
        moved=moved,
    )
    prefixes = call(
        functools.partial(prefix_kernel, group, matchings),
        [body] * group,
        (weight1, *packets, *earlier),
        "prefix_states",
        scratch=[pltpu.VMEM((group * PACKET, LANES), bf16), pltpu.VMEM((group * BODY, LANES), bf16)],
    )
    states = trade(prefixes)
    (weight2,) = call(
        functools.partial(load_kernel, width),
        [third],
        (prefixes[0], out_weight),
        "weight_load",
        scratch=[dma((loads,))],
        far_in=(1,),
        moved=moved,
    )
    (hidden,) = call(
        functools.partial(hidden_kernel, group),
        [jax.ShapeDtypeStruct((rows, width + LANES), bf16)],
        (opened, intra, scale, weight2, *states),
        "hidden",
    )
    others = [
        lax.ppermute(hidden, "tp", [(i, (i + k) % parts) for i in range(parts)])
        for k in range(1, parts)
    ]
    (near,) = call(
        near_kernel,
        [jax.ShapeDtypeStruct((rows, features), f32)],
        (hidden, weight0, weight1, weight2),
        "near",
        flops=2 * rows * width * features,
        moved=2 * width * features,
    )
    (out,) = call(
        functools.partial(far_kernel, parts),
        [jax.ShapeDtypeStruct((rows, features), bf16)],
        (near, weight0, weight1, weight2, hidden, *others),
        "far",
        scratch=[pltpu.VMEM((rows, features), bf16), dma((6,))],
        far_out=(0,),
        flops=2 * rows * width * features,
        moved=2 * width * features,
    )
    return out


def solution(mesh):
    return jax.shard_map(
        on_device,
        mesh=mesh,
        in_specs=(
            P("seq", "tp"),
            P("seq", "tp"),
            P("seq", "tp"),
            P("seq", "tp"),
            P(),
            P("seq"),
            P(None, "tp"),
        ),
        out_specs=P("seq", "tp"),
        check_vma=False,
    )
```
